256 devices in a mesh: heads: 8 (over x, core), seq: 32 (over y, z).
Axes of the slice: x: 4, y: 4, z: 8, core: 2. Of those that a mesh axis runs over, the one named last changes fastest.
Arguments:
- tokens: bfloat16 [8192, 4096], P('seq'), may hold values from -6 to 6
- norm_gain: float32 [4096], replicated, may hold values from 0.1 to 1.9
- w_query: bfloat16 [4096, 4096], P(None, 'heads'), may hold values from -0.09375 to 0.09375
- w_key: bfloat16 [4096, 1024], P(None, 'heads'), may hold values from -0.1875 to 0.1875
- w_value: bfloat16 [4096, 1024], P(None, 'heads'), may hold values from -0.375 to 0.375
- w_out: bfloat16 [4096, 4096], P('heads'), may hold values from -0.09375 to 0.09375
- cache_keys: bfloat16 [8, 32768, 128], P('heads', 'seq'), may hold values from -360 to 360
- cache_values: bfloat16 [8, 32768, 128], P('heads', 'seq'), may hold values from -24 to 24
- vert_blocks: int32 [8, 64], P('heads'), may hold values from -1 to 511, as said below
- vert_count: int32 [8], P('heads'), may hold values from 32 to 64
- slash_offsets: int32 [8, 4], P('heads'), may hold values from -1 to 4, as said below
- slash_count: int32 [8], P('heads'), may hold values from 1 to 4
Outputs:
- layer_out: bfloat16 [8192, 4096], P('seq', 'heads')
The draws below stay inside these ranges and needn't reach their ends.
Inputs may be any that keep to these rules, and one draw needn't show every extreme that they name: `vert_blocks`: row g lists cache blocks for key/value head g: its entries before vert_count[g] are distinct, the rest are -1. The cache of one index of seq holds at most 8 of the blocks that a row lists, and exactly 8 for one index in every row. `slash_offsets`: entries of row g before slash_count[g] are distinct, the rest are -1.
All inputs are finite; a program needn't handle non-finite values.
Results may differ from the reference program's by a relative error of at most 0.015.
The reference program's roundings to bfloat16 on the way count: a program that leaves them out, or rounds other values in their place, can miss the bound.
Values may be sent and summed in bfloat16 or wider, within the bound.
No kernel may reach another device: no remote copies, remote signals or barrier semaphores. Data moves between devices by JAX's collectives and lax.ppermute only.
A program may use at most 64 MiB of HBM per device.

```python
import math
import jax
import jax.numpy as jnp
from jax import lax

D = 4096
QH = 32
KVH = 8
HD = 128
BLK = 64
NV = 64
VCAP = 8
SMAX = 4
CACHE_DEV = 1024
TOKENS = 8192
CACHE = 32768


def vertical_lists(key):
    base_key = jax.random.fold_in(key, 7)
    count_key, pick_key, hot_key, order_key, tie_key, mix_key = jax.random.split(base_key, 6)
    device_total = CACHE // CACHE_DEV
    per_device = CACHE_DEV // BLK
    counts = jax.random.randint(count_key, (KVH,), NV // 2, NV + 1)
    chosen_heads = jax.random.permutation(pick_key, KVH)
    counts = counts.at[chosen_heads[0]].set(NV).at[chosen_heads[1]].set(NV // 2)
    hot_device = jax.random.randint(hot_key, (KVH,), 0, device_total)
    order_scores = jax.random.randint(order_key, (KVH, device_total, per_device), 0, 2 ** 16) * per_device + jnp.arange(per_device)
    block_order = jnp.argsort(order_scores, axis=-1, stable=True)[:, :, :VCAP]
    candidate = jnp.arange(device_total)[None, :, None] * per_device + block_order
    hot_device_mask = jnp.arange(device_total)[None, :] == hot_device[:, None]
    priority = jnp.where(hot_device_mask[:, :, None], 0, 1 + jnp.arange(VCAP)[None, None, :])
    tie_break = jax.random.randint(tie_key, (KVH, device_total, VCAP), 0, 1024)
    flat_index = jnp.arange(device_total * VCAP).reshape(device_total, VCAP)[None]
    ranking = (priority * 1024 + tie_break) * (device_total * VCAP) + flat_index
    pick_order = jnp.argsort(ranking.reshape(KVH, -1), axis=-1, stable=True)[:, :NV]
    picked = jnp.take_along_axis(candidate.reshape(KVH, -1), pick_order, axis=1)
    positions = jnp.arange(NV)[None, :]
    live_entry = positions < counts[:, None]
    mixing = jnp.where(live_entry, jax.random.randint(mix_key, (KVH, NV), 0, 2 ** 12) * NV + positions, 2 ** 22 + positions)
    shuffle = jnp.argsort(mixing, axis=-1, stable=True)
    block_lists = jnp.take_along_axis(picked, shuffle, axis=1)
    return (jnp.where(live_entry, block_lists, -1).astype(jnp.int32), counts.astype(jnp.int32))


def slash_lists(key):
    base_key = jax.random.fold_in(key, 11)
    count_key, pick_key, order_key = jax.random.split(base_key, 3)
    counts = jax.random.randint(count_key, (KVH,), 1, SMAX + 1)
    chosen_heads = jax.random.permutation(pick_key, KVH)
    counts = counts.at[chosen_heads[0]].set(SMAX).at[chosen_heads[1]].set(1)
    scores = jax.random.randint(order_key, (KVH, SMAX), 0, 2 ** 16) * SMAX + jnp.arange(SMAX)
    offsets = jnp.argsort(scores, axis=-1, stable=True) + 1
    live_entry = jnp.arange(SMAX)[None, :] < counts[:, None]
    return (jnp.where(live_entry, offsets, -1).astype(jnp.int32), counts.astype(jnp.int32))


def draw_vert_blocks(key, part):
    return vertical_lists(key)[0]


def draw_vert_count(key, part):
    return vertical_lists(key)[1]


def draw_slash_offsets(key, part):
    return slash_lists(key)[0]


def draw_slash_count(key, part):
    return slash_lists(key)[1]


def draw_cache_keys(key, part):
    noise_key = jax.random.fold_in(jax.random.fold_in(key, 3), 0)
    values = jnp.clip(jax.random.normal(noise_key, (KVH, CACHE, HD), jnp.float32), -6.0, 6.0) * 2.0
    return values.astype(jnp.bfloat16)


def block_levels(own_key, shape, pieces, least, largest):
    level = 1.0
    for dim, shards_of in pieces:
        draws = jax.random.uniform(jax.random.fold_in(jax.random.fold_in(own_key, 6), dim), (shards_of,), jnp.float32, least / len(pieces), largest / len(pieces))
        level = level * jnp.repeat(jnp.exp(draws), shape[dim] // shards_of).reshape((-1,) + (1,) * (len(shape) - 1 - dim))
    return level


def noise(rng, shape, deviation, limit, pieces=(), held_as=jnp.bfloat16):
    drawn = jax.random.normal(rng, shape, jnp.float32) * deviation
    if len(pieces) > 0:
        drawn = block_levels(rng, shape, pieces, -0.22, 0.18) * drawn
    return jnp.clip(drawn, min=-limit, max=limit).astype(held_as)


def setup_inputs(seed: int = 0) -> dict:
    key_list = jax.random.split(jax.random.key(seed), 13)
    return {
        "tokens": noise(key_list[0], (TOKENS, D), 1.0, 6.0, ((0, 32),)),
        "norm_gain": jnp.clip(1.0 + 0.18 * jax.random.normal(key_list[1], (D,), jnp.float32), 0.1, 1.9),
        "w_query": noise(key_list[2], (D, QH * HD), D ** -0.5, 0.09375, ((1, 8),)),
        "w_key": noise(key_list[3], (D, KVH * HD), (D // 4) ** -0.5, 0.1875, ((1, 8),)),
        "w_value": noise(key_list[4], (D, KVH * HD), (D // 16) ** -0.5, 0.375, ((1, 8),)),
        "w_out": noise(key_list[5], (QH * HD, D), (QH * HD) ** -0.5, 0.09375, ((0, 8),)),
        "cache_keys": draw_cache_keys(jax.random.fold_in(key_list[12], 71), 0),
        "cache_values": noise(key_list[7], (KVH, CACHE, HD), 4.0, 24.0, ((0, 8), (1, 32))),
        "vert_blocks": draw_vert_blocks(jax.random.fold_in(key_list[12], 71), 0),
        "vert_count": draw_vert_count(jax.random.fold_in(key_list[12], 71), 0),
        "slash_offsets": draw_slash_offsets(jax.random.fold_in(key_list[12], 71), 0),
        "slash_count": draw_slash_count(jax.random.fold_in(key_list[12], 71), 0),
    }


def reference(tokens, norm_gain, w_query, w_key, w_value, w_out, cache_keys, cache_values, vert_blocks, vert_count, slash_offsets, slash_count):
    activation = tokens.astype(jnp.float32)
    normed = (activation * lax.rsqrt(lax.optimization_barrier(jnp.mean(activation * activation, axis=-1, keepdims=True)) + 1e-05) * norm_gain).astype(jnp.bfloat16)
    queries = jnp.dot(normed, w_query, preferred_element_type=jnp.float32).astype(jnp.bfloat16)
    key_rows = jnp.dot(normed, w_key, preferred_element_type=jnp.float32).astype(jnp.bfloat16)
    value_rows = jnp.dot(normed, w_value, preferred_element_type=jnp.float32).astype(jnp.bfloat16)
    group_size = QH // KVH
    score_scale = 1.0 / math.sqrt(HD)
    query_blocks = TOKENS // BLK
    head_queries = queries.reshape(TOKENS, QH, HD).transpose(1, 0, 2)
    new_keys = key_rows.reshape(TOKENS, KVH, HD).transpose(1, 0, 2).reshape(KVH, query_blocks, BLK, HD)
    new_values = value_rows.reshape(TOKENS, KVH, HD).transpose(1, 0, 2).reshape(KVH, query_blocks, BLK, HD)
    cache_key_blocks = cache_keys.reshape(KVH, CACHE // BLK, BLK, HD)
    cache_value_blocks = cache_values.reshape(KVH, CACHE // BLK, BLK, HD)
    offsets_all = jnp.arange(SMAX + 1)
    inner_row = jnp.arange(BLK)

    def one_head(head_index):
        shared_head = head_index // group_size
        query_rows = head_queries[head_index]
        live_entry = jnp.arange(NV) < vert_count[shared_head]
        picked = jnp.clip(vert_blocks[shared_head], 0, CACHE // BLK - 1)
        far_keys = jnp.take(cache_key_blocks[shared_head], picked, axis=0).reshape(NV * BLK, HD)
        far_values = jnp.take(cache_value_blocks[shared_head], picked, axis=0).reshape(NV * BLK, HD)
        far_scores = jnp.dot(query_rows, far_keys.T, preferred_element_type=jnp.float32) * score_scale
        far_scores = jnp.where(jnp.repeat(live_entry, BLK)[None, :], far_scores, -jnp.inf)
        padded_keys = jnp.concatenate([jnp.zeros((SMAX, BLK, HD), jnp.bfloat16), new_keys[shared_head]], 0)
        padded_values = jnp.concatenate([jnp.zeros((SMAX, BLK, HD), jnp.bfloat16), new_values[shared_head]], 0)
        window_keys = jnp.stack([padded_keys[SMAX - offset:SMAX - offset + query_blocks] for offset in range(SMAX + 1)], 0)
        window_values = jnp.stack([padded_values[SMAX - offset:SMAX - offset + query_blocks] for offset in range(SMAX + 1)], 0)
        blocked_queries = query_rows.reshape(query_blocks, BLK, HD).astype(jnp.float32)
        near_scores = jnp.einsum('bih,objh->bioj', blocked_queries, window_keys.astype(jnp.float32)) * score_scale
        slash_hit = jnp.any((slash_offsets[shared_head][None, :] == offsets_all[:, None]) & (jnp.arange(SMAX)[None, :] < slash_count[shared_head]), axis=1)
        exists = jnp.arange(query_blocks)[:, None] - offsets_all[None, :] >= 0
        causal = inner_row[:, None] >= inner_row[None, :]
        allowed = exists[:, None, :, None] & (slash_hit[None, None, :, None] | (offsets_all == 0)[None, None, :, None] & causal[None, :, None, :])
        near_scores = jnp.where(allowed, near_scores, -jnp.inf).reshape(TOKENS, (SMAX + 1) * BLK)
        row_max = jnp.maximum(lax.optimization_barrier(jnp.max(far_scores, axis=1)), lax.optimization_barrier(jnp.max(near_scores, axis=1)))
        far_weights = jnp.exp(far_scores - row_max[:, None])
        near_weights = jnp.exp(near_scores - row_max[:, None])
        weight_sum = lax.optimization_barrier(jnp.sum(far_weights, axis=1)) + lax.optimization_barrier(jnp.sum(near_weights, axis=1))
        mixed_out = jnp.dot(far_weights.astype(jnp.bfloat16), far_values, preferred_element_type=jnp.float32)
        near_rounded = near_weights.astype(jnp.bfloat16).astype(jnp.float32).reshape(query_blocks, BLK, SMAX + 1, BLK)
        mixed_out = mixed_out + jnp.einsum('bioj,objh->bih', near_rounded, window_values.astype(jnp.float32)).reshape(TOKENS, HD)
        return (mixed_out / weight_sum[:, None]).astype(jnp.bfloat16)
    attended = lax.map(one_head, jnp.arange(QH))
    attended = attended.transpose(1, 0, 2).reshape(TOKENS, QH * HD)
    return jnp.dot(attended, w_out, preferred_element_type=jnp.float32).astype(jnp.bfloat16)
```

```python
import functools
import math

import jax
import jax.numpy as jnp
from jax import lax
from jax.experimental import pallas as pl
from jax.experimental.pallas import tpu as pltpu
from jax.sharding import PartitionSpec as P

BLK = 64
HD = 128
GROUP = 4
NY = 4
NZ = 8
NX = 4
VMEM = pltpu.VMEM
VSPEC = pl.BlockSpec(memory_space=pltpu.VMEM)
SSPEC = pl.BlockSpec(memory_space=pltpu.SMEM)
SCALE2 = math.log2(math.e) / math.sqrt(HD)
NEG = -jnp.inf


def params(mib):
    return pltpu.CompilerParams(vmem_limit_bytes=mib << 20)


def shift_y(block, d):
    return lax.ppermute(
        block, "seq", [(y * NZ + z, (y + d) % NY * NZ + z) for y in range(NY) for z in range(NZ)]
    )


def shift_z(block, d):
    return lax.ppermute(
        block, "seq", [(y * NZ + z, y * NZ + (z + d) % NZ) for y in range(NY) for z in range(NZ)]
    )


def shift_x(block, d):
    return lax.ppermute(
        block, "heads", [(2 * x + c, 2 * ((x + d) % NX) + c) for x in range(NX) for c in range(2)]
    )


def swap_core(block):
    return lax.ppermute(block, "heads", [(i, i ^ 1) for i in range(2 * NX)])


def position():
    me = lax.axis_index("seq")
    return me // NZ, lax.rem(me, NZ)


def pick_kernel(tab, cs, ck, cv, *outs):
    y, z = position()
    group = z * NY + y
    start = cs[group]
    size = cs[group + 1] - start
    for dy in range(NY):
        for j in range(2):
            i = ((y + dy - start) & 3) + 4 * j
            entry = tab[jnp.minimum(start + i, 63)]
            row = pl.multiple_of(jnp.where(i < size, entry & 15, 0) * BLK, BLK)
            outs[dy][j, 0] = ck[0, pl.ds(row, BLK), :]
            outs[dy][j, 1] = cv[0, pl.ds(row, BLK), :]


def column_kernel(tab, cs, r0, r1, r2, r3, out):
    y, z = position()
    recv = (r0, r1, r2, r3)
    start = cs[z * NY]
    size = cs[z * NY + NY] - start
    first = (y - start) & 3
    for i in range(8):
        off = first + 4 * i
        live = off < size
        r = jnp.minimum(start + off, 63)
        entry = tab[r]
        hy = (entry >> 4) & 3
        j = jnp.where(live, (r - cs[z * NY + hy]) >> 2, 0)
        d = jnp.where(live, (y - hy) & 3, 0)
        for k in range(NY):

            @pl.when(d == k)
            def _():
                out[i] = recv[k][j]


def row_kernel(tab, cs, count, *refs):
    y, z = position()
    recv, out = refs[:NZ], refs[NZ]
    for m in range(16):
        r = y + 4 * m
        live = r < count[0]
        entry = tab[r]
        zs = jnp.where(live, entry >> 6, z)
        start = cs[zs * NY]
        first = (y - start) & 3
        i = jnp.where(live, (r - start - first) >> 2, 0)
        d = (z - zs) & 7
        for k in range(NZ):

            @pl.when(d == k)
            def _():
                out[0, m * BLK : (m + 1) * BLK] = recv[k][i, 0]
                out[1, m * BLK : (m + 1) * BLK] = recv[k][i, 1]


def near_kernel(offs, cnt, q, kp, vp, k, v, m_out, l_out, acc_out):
    me = lax.axis_index("seq")
    rows = k.shape[0]
    keys = jnp.concatenate([kp[...], k[...]], axis=0)
    values = jnp.concatenate([vp[...], v[...]], axis=0)
    t = lax.broadcasted_iota(jnp.int32, (rows, 2 * rows), 0)
    u = lax.broadcasted_iota(jnp.int32, (rows, 2 * rows), 1) - rows
    gap = (t >> 6) - (u >> 6)
    hit = (gap == 0) & (u <= t)
    for e in range(4):
        off = jnp.where((e < cnt[0]) & (offs[0, e] >= 0), offs[0, e], -100)
        hit = hit | (gap == off)
    hit = hit & (u >= jnp.where(me > 0, -rows, 0))
    for h in range(GROUP):
        s = lax.dot_general(
            q[:, h * HD : (h + 1) * HD],
            keys,
            (((1,), (1,)), ((), ())),
            preferred_element_type=jnp.float32,
        )
        s = jnp.where(hit, s, NEG)
        top = jnp.max(s, axis=1, keepdims=True)
        p = jnp.exp2((s - top) * SCALE2)
        m_out[h] = jnp.broadcast_to(top, (rows, HD))
        l_out[h] = jnp.broadcast_to(jnp.sum(p, axis=1, keepdims=True), (rows, HD))
        acc_out[h] = jnp.dot(p.astype(jnp.bfloat16), values, preferred_element_type=jnp.float32)


def far_step(count, shift, q, kv, m_in, l_in, acc_in, h):
    y, _ = position()
    src = (y - shift) & 3
    live = ((count[0] - src + 3) >> 2) * BLK
    s = lax.dot_general(
        q[:, h * HD : (h + 1) * HD],
        kv[0],
        (((1,), (1,)), ((), ())),
        preferred_element_type=jnp.float32,
    )
    key = lax.broadcasted_iota(jnp.int32, s.shape, 1)
    s = jnp.where(key < live, s, NEG)
    old = m_in[h][:, :1]
    top = jnp.maximum(old, jnp.max(s, axis=1, keepdims=True))
    factor = jnp.exp2((old - top) * SCALE2)
    p = jnp.exp2((s - top) * SCALE2)
    total = l_in[h][:, :1] * factor + jnp.sum(p, axis=1, keepdims=True)
    acc = acc_in[h] * factor + jnp.dot(
        p.astype(jnp.bfloat16), kv[1], preferred_element_type=jnp.float32
    )
    return top, total, acc


def far_kernel(shift, count, q, kv, m_in, l_in, acc_in, m_out, l_out, acc_out):
    for h in range(GROUP):
        top, total, acc = far_step(count, shift, q, kv, m_in, l_in, acc_in, h)
        m_out[h] = jnp.broadcast_to(top, m_out.shape[1:])
        l_out[h] = jnp.broadcast_to(total, l_out.shape[1:])
        acc_out[h] = acc


def last_kernel(shift, count, q, kv, m_in, l_in, acc_in, att):
    for h in range(GROUP):
        _, total, acc = far_step(count, shift, q, kv, m_in, l_in, acc_in, h)
        att[:, h * HD : (h + 1) * HD] = (acc / total).astype(jnp.bfloat16)


def away_kernel(cols, att, w, out):
    out[0] = jnp.dot(att[...], w[...], preferred_element_type=jnp.float32).astype(out.dtype)


def home_kernel(cols, att, w, recv, out):
    mine = jnp.dot(att[...], w[...], preferred_element_type=jnp.float32)
    out[...] = (mine + recv[0].astype(jnp.float32)).astype(out.dtype)


def final_kernel(mine, a, b, c, out):
    total = mine[...] + a[...].astype(jnp.float32)
    total = total + b[...].astype(jnp.float32) + c[...].astype(jnp.float32)
    out[...] = total.astype(out.dtype)


def local(
    tokens,
    norm_gain,
    w_query,
    w_key,
    w_value,
    w_out,
    cache_keys,
    cache_values,
    vert_blocks,
    vert_count,
    slash_offsets,
    slash_count,
):
    rows = tokens.shape[0]
    bf16 = jnp.bfloat16
    f32 = jnp.float32
    blocks = vert_blocks[0]
    entry = jnp.arange(64, dtype=jnp.int32)
    key = jnp.where(
        entry < vert_count[0],
        (((blocks >> 4) & 7) << 6) | ((blocks >> 7) << 4) | (blocks & 15),
        4096 + entry,
    )
    edges = jnp.concatenate([key, jnp.arange(64, dtype=jnp.int32) * 16])
    below = jnp.sum((key[None, :] < edges[:, None]).astype(jnp.int32), axis=1)
    rank, cs = below[:64], below[64:]
    tab = jnp.sum(jnp.where(rank[None, :] == entry[:, None], key[None, :], 0), axis=1)

    slot = jax.ShapeDtypeStruct((2, 2, BLK, HD), bf16)
    picked = pl.pallas_call(
        pick_kernel,
        out_shape=[slot] * NY,
        in_specs=[SSPEC, SSPEC, VSPEC, VSPEC],
        out_specs=[VSPEC] * NY,
        compiler_params=params(8),
        name="pick",
    )(tab, cs, cache_keys, cache_values)
    spread = [picked[0]] + [shift_y(picked[d], d) for d in range(1, NY)]
    column = pl.pallas_call(
        column_kernel,
        out_shape=jax.ShapeDtypeStruct((8, 2, BLK, HD), bf16),
        in_specs=[SSPEC, SSPEC] + [VSPEC] * NY,
        out_specs=VSPEC,
        compiler_params=params(8),
        name="column",
    )(tab, cs, *spread)
    ring = [column] + [None] * 7
    ring[1], ring[7] = shift_z(column, 1), shift_z(column, -1)
    ring[2], ring[6] = shift_z(ring[1], 1), shift_z(ring[7], -1)
    ring[3], ring[5] = shift_z(ring[2], 1), shift_z(ring[6], -1)
    ring[4] = shift_z(ring[3], 1)
    own = pl.pallas_call(
        row_kernel,
        out_shape=jax.ShapeDtypeStruct((2, 16 * BLK, HD), bf16),
        in_specs=[SSPEC] * 3 + [VSPEC] * NZ,
        out_specs=VSPEC,
        compiler_params=params(16),
        name="row",
    )(tab, cs, vert_count, *ring)
    parts = [own] + [shift_y(own, d) for d in (1, 3, 2)]

    activation = tokens.astype(f32)
    normed = (
        activation
        * lax.rsqrt(jnp.mean(activation * activation, axis=-1, keepdims=True) + 1e-05)
        * norm_gain
    ).astype(bf16)
    key_rows = jnp.dot(normed, w_key, preferred_element_type=f32).astype(bf16)
    value_rows = jnp.dot(normed, w_value, preferred_element_type=f32).astype(bf16)
    seqs = lax.axis_size("seq")
    route = [(i, (i + 1) % seqs) for i in range(seqs)]
    before_keys, before_values = lax.ppermute((key_rows, value_rows), "seq", route)
    queries = jnp.dot(normed, w_query, preferred_element_type=f32).astype(bf16)

    state_shape = [jax.ShapeDtypeStruct((GROUP, rows, HD), f32)] * 3
    state = pl.pallas_call(
        near_kernel,
        out_shape=state_shape,
        in_specs=[SSPEC] * 2 + [VSPEC] * 5,
        out_specs=[VSPEC] * 3,
        compiler_params=params(24),
        name="near",
    )(slash_offsets, slash_count, queries, before_keys, before_values, key_rows, value_rows)
    for shift, part in zip((0, 1, 3), parts):
        state = pl.pallas_call(
            functools.partial(far_kernel, shift),
            out_shape=state_shape,
            in_specs=[SSPEC] + [VSPEC] * 5,
            out_specs=[VSPEC] * 3,
            compiler_params=params(24),
            name="far",
        )(vert_count, queries, part, *state)
    attended = pl.pallas_call(
        functools.partial(last_kernel, 2),
        out_shape=jax.ShapeDtypeStruct((rows, GROUP * HD), bf16),
        in_specs=[SSPEC] + [VSPEC] * 5,
        out_specs=VSPEC,
        compiler_params=params(24),
        name="last",
    )(vert_count, queries, parts[3], *state)

    heads = lax.axis_index("heads")
    x, core = heads // 2, lax.rem(heads, 2)
    depth = GROUP * HD
    order = (x + jnp.arange(NX, dtype=jnp.int32)) & 3
    away = pl.pallas_call(
        away_kernel,
        out_shape=jax.ShapeDtypeStruct((NX, rows, depth), bf16),
        grid_spec=pltpu.PrefetchScalarGridSpec(
            num_scalar_prefetch=1,
            grid=(NX,),
            in_specs=[
                pl.BlockSpec((rows, depth), lambda i, cols: (0, 0)),
                pl.BlockSpec((depth, depth), lambda i, cols: (0, cols[i])),
            ],
            out_specs=pl.BlockSpec((1, rows, depth), lambda i, cols: (i, 0, 0)),
        ),
        compiler_params=params(16),
        name="away",
    )(order * 2 + 1 - core, attended, w_out)
    recv = swap_core(away)
    home_cols = order * 2 + core

    def home(d, dtype):
        return pl.pallas_call(
            home_kernel,
            out_shape=jax.ShapeDtypeStruct((rows, depth), dtype),
            grid_spec=pltpu.PrefetchScalarGridSpec(
                num_scalar_prefetch=1,
                grid=(1,),
                in_specs=[
                    pl.BlockSpec((rows, depth), lambda i, cols: (0, 0)),
                    pl.BlockSpec((depth, depth), lambda i, cols: (0, cols[d])),
                    pl.BlockSpec((1, rows, depth), lambda i, cols: (d, 0, 0)),
                ],
                out_specs=pl.BlockSpec((rows, depth), lambda i, cols: (0, 0)),
            ),
            compiler_params=params(16),
            name="home",
        )(home_cols, attended, w_out, recv)

    sums = [shift_x(home(d, bf16), d) for d in (2, 1, 3)]
    return pl.pallas_call(
        final_kernel,
        out_shape=jax.ShapeDtypeStruct((rows, depth), bf16),
        in_specs=[VSPEC] * 4,
        out_specs=VSPEC,
        compiler_params=params(16),
        name="final",
    )(home(0, f32), *sums)


def solution(mesh):
    return jax.shard_map(
        local,
        mesh=mesh,
        in_specs=(
            P("seq", None),
            P(),
            P(None, "heads"),
            P(None, "heads"),
            P(None, "heads"),
            P("heads", None),
            P("heads", "seq", None),
            P("heads", "seq", None),
            P("heads", None),
            P("heads"),
            P("heads", None),
            P("heads"),
        ),
        out_specs=P("seq", "heads"),
        check_vma=False,
    )
```

```python
import functools
import math

import jax
import jax.numpy as jnp
from jax import lax
from jax.experimental import pallas as pl
from jax.experimental.pallas import tpu as pltpu
from jax.sharding import PartitionSpec as P

BLK = 64
HD = 128
GROUP = 4
NY = 4
NZ = 8
NX = 4
VMEM = pltpu.VMEM
VSPEC = pl.BlockSpec(memory_space=pltpu.VMEM)
SSPEC = pl.BlockSpec(memory_space=pltpu.SMEM)
SCALE2 = math.log2(math.e) / math.sqrt(HD)
NEG = -jnp.inf


def params(mib):
    return pltpu.CompilerParams(vmem_limit_bytes=mib << 20)


def cost(us):
    return pl.CostEstimate(flops=int(us * 1e9), bytes_accessed=0, transcendentals=0)


def tie(*values):
    return lax.optimization_barrier(values)


def shift_y(block, d):
    return lax.ppermute(
        block, "seq", [(y * NZ + z, (y + d) % NY * NZ + z) for y in range(NY) for z in range(NZ)]
    )


def shift_z(block, d):
    return lax.ppermute(
        block, "seq", [(y * NZ + z, y * NZ + (z + d) % NZ) for y in range(NY) for z in range(NZ)]
    )


def shift_x(block, d):
    return lax.ppermute(
        block, "heads", [(2 * x + c, 2 * ((x + d) % NX) + c) for x in range(NX) for c in range(2)]
    )


def swap_core(block):
    return lax.ppermute(block, "heads", [(i, i ^ 1) for i in range(2 * NX)])


def position():
    me = lax.axis_index("seq")
    return me // NZ, lax.rem(me, NZ)


def at(tab, group):
    return tab[64 + group]


def pick_kernel(tab, ck, cv, *outs):
    y, z = position()
    group = z * NY + y
    start = at(tab, group)
    size = at(tab, group + 1) - start
    for dy in range(NY):
        for j in range(2):
            i = ((y + dy - start) & 3) + 4 * j
            entry = tab[jnp.minimum(start + i, 63)]
            row = pl.multiple_of(jnp.where(i < size, entry & 15, 0) * BLK, BLK)
            outs[dy][j, 0] = ck[0, pl.ds(row, BLK), :]
            outs[dy][j, 1] = cv[0, pl.ds(row, BLK), :]


def column_kernel(tab, r0, r1, r2, r3, out):
    y, z = position()
    recv = (r0, r1, r2, r3)
    start = at(tab, z * NY)
    size = at(tab, z * NY + NY) - start
    first = (y - start) & 3
    for i in range(8):
        off = first + 4 * i
        live = off < size
        r = jnp.minimum(start + off, 63)
        hy = (tab[r] >> 4) & 3
        j = jnp.where(live, (r - at(tab, z * NY + hy)) >> 2, 0)
        d = jnp.where(live, (y - hy) & 3, 0)
        for k in range(NY):

            @pl.when(d == k)
            def _():
                out[i] = recv[k][j]


def row_kernel(tab, *refs):
    y, z = position()
    recv, outs = refs[:NZ], refs[NZ:]
    for m in range(16):
        r = y + 4 * m
        live = r < at(tab, 32)
        zs = jnp.where(live, tab[r] >> 6, z)
        start = at(tab, zs * NY)
        first = (y - start) & 3
        i = jnp.where(live, (r - start - first) >> 2, 0)
        d = (z - zs) & 7
        out, place = outs[m // 8], m % 8 * BLK
        for k in range(NZ):

            @pl.when(d == k)
            def _():
                out[0, place : place + BLK] = recv[k][i, 0]
                out[1, place : place + BLK] = recv[k][i, 1]


def near_kernel(offs, cnt, q, kp, vp, k, v, m_out, l_out, acc_out):
    me = lax.axis_index("seq")
    rows = k.shape[0]
    keys = jnp.concatenate([kp[...], k[...]], axis=0)
    values = jnp.concatenate([vp[...], v[...]], axis=0)
    t = lax.broadcasted_iota(jnp.int32, (rows, 2 * rows), 0)
    u = lax.broadcasted_iota(jnp.int32, (rows, 2 * rows), 1) - rows
    gap = (t >> 6) - (u >> 6)
    hit = (gap == 0) & (u <= t)
    for e in range(4):
        off = jnp.where((e < cnt[0]) & (offs[0, e] >= 0), offs[0, e], -100)
        hit = hit | (gap == off)
    hit = hit & (u >= jnp.where(me > 0, -rows, 0))
    for h in range(GROUP):
        s = lax.dot_general(
            q[:, h * HD : (h + 1) * HD],
            keys,
            (((1,), (1,)), ((), ())),
            preferred_element_type=jnp.float32,
        )
        s = jnp.where(hit, s, NEG)
        top = jnp.max(s, axis=1, keepdims=True)
        p = jnp.exp2((s - top) * SCALE2)
        m_out[h] = jnp.broadcast_to(top, (rows, HD))
        l_out[h] = jnp.broadcast_to(jnp.sum(p, axis=1, keepdims=True), (rows, HD))
        acc_out[h] = jnp.dot(p.astype(jnp.bfloat16), values, preferred_element_type=jnp.float32)


def far_step(live, q, lo, hi, m_in, l_in, acc_in, h):
    def scores(kv, base):
        s = lax.dot_general(
            q[:, h * HD : (h + 1) * HD],
            kv[0],
            (((1,), (1,)), ((), ())),
            preferred_element_type=jnp.float32,
        )
        key = base + lax.broadcasted_iota(jnp.int32, s.shape, 1)
        return jnp.where(key < live, s, NEG)

    s0, s1 = scores(lo, 0), scores(hi, lo.shape[1])
    old = m_in[h][:, :1]
    top = jnp.maximum(
        old,
        jnp.maximum(jnp.max(s0, axis=1, keepdims=True), jnp.max(s1, axis=1, keepdims=True)),
    )
    factor = jnp.exp2((old - top) * SCALE2)
    p0 = jnp.exp2((s0 - top) * SCALE2)
    p1 = jnp.exp2((s1 - top) * SCALE2)
    total = (
        l_in[h][:, :1] * factor
        + jnp.sum(p0, axis=1, keepdims=True)
        + jnp.sum(p1, axis=1, keepdims=True)
    )
    acc = (
        acc_in[h] * factor
        + jnp.dot(p0.astype(jnp.bfloat16), lo[1], preferred_element_type=jnp.float32)
        + jnp.dot(p1.astype(jnp.bfloat16), hi[1], preferred_element_type=jnp.float32)
    )
    return top, total, acc


def live_keys(tab, shift):
    y, _ = position()
    return ((at(tab, 32) - ((y - shift) & 3) + 3) >> 2) * BLK


def far_kernel(shift, tab, q, lo, hi, m_in, l_in, acc_in, m_out, l_out, acc_out):
    live = live_keys(tab, shift)
    for h in range(GROUP):
        top, total, acc = far_step(live, q, lo, hi, m_in, l_in, acc_in, h)
        m_out[h] = jnp.broadcast_to(top, m_out.shape[1:])
        l_out[h] = jnp.broadcast_to(total, l_out.shape[1:])
        acc_out[h] = acc


def last_kernel(shift, tab, q, lo, hi, m_in, l_in, acc_in, att):
    live = live_keys(tab, shift)
    for h in range(GROUP):
        _, total, acc = far_step(live, q, lo, hi, m_in, l_in, acc_in, h)
        att[:, h * HD : (h + 1) * HD] = (acc / total).astype(jnp.bfloat16)


def away_kernel(cols, att, w, out):
    out[0] = jnp.dot(att[...], w[...], preferred_element_type=jnp.float32).astype(out.dtype)


def home_kernel(cols, att, w, recv, out):
    mine = jnp.dot(att[...], w[...], preferred_element_type=jnp.float32)
    out[0] = mine + recv[0].astype(jnp.float32)


def halves_kernel(cols, att, w, recv, a, b):
    mine = jnp.dot(att[...], w[...], preferred_element_type=jnp.float32)
    total = (mine + recv[0].astype(jnp.float32)).astype(a.dtype)
    half = a.shape[0]
    a[...] = total[:half]
    b[...] = total[half:]


def pass_kernel(home, a, b, right, left):
    half = a.shape[0]
    right[:half] = (home[1, :half] + a[...].astype(jnp.float32)).astype(right.dtype)
    right[half:] = home[1, half:].astype(right.dtype)
    left[:half] = home[2, :half].astype(left.dtype)
    left[half:] = (home[2, half:] + b[...].astype(jnp.float32)).astype(left.dtype)


def final_kernel(home, a, b, out):
    total = home[0] + a[...].astype(jnp.float32) + b[...].astype(jnp.float32)
    out[...] = total.astype(out.dtype)


def local(
    tokens,
    norm_gain,
    w_query,
    w_key,
    w_value,
    w_out,
    cache_keys,
    cache_values,
    vert_blocks,
    vert_count,
    slash_offsets,
    slash_count,
):
    rows = tokens.shape[0]
    bf16 = jnp.bfloat16
    f32 = jnp.float32
    blocks = vert_blocks[0]
    index = jnp.arange(128, dtype=jnp.int32)
    entry = index[:64]
    key = jnp.where(
        entry < vert_count[0],
        (((blocks >> 4) & 7) << 6) | ((blocks >> 7) << 4) | (blocks & 15),
        4096 + entry,
    )
    edges = jnp.concatenate([key, entry * 16])
    below = jnp.sum((key[None, :] < edges[:, None]).astype(jnp.int32), axis=1)
    ranked = jnp.sum(jnp.where(below[None, :64] == index[:, None], key[None, :], 0), axis=1)
    tab = jnp.where(index < 64, ranked, below)

    slot = jax.ShapeDtypeStruct((2, 2, BLK, HD), bf16)
    picked = pl.pallas_call(
        pick_kernel,
        out_shape=[slot] * NY,
        in_specs=[SSPEC, VSPEC, VSPEC],
        out_specs=[VSPEC] * NY,
        compiler_params=params(8),
        cost_estimate=cost(0.7),
        name="pick",
    )(tab, cache_keys, cache_values)
    spread = [picked[0]] + [shift_y(picked[d], d) for d in range(1, NY)]
    activation = tokens.astype(f32)
    normed = (
        activation
        * lax.rsqrt(jnp.mean(activation * activation, axis=-1, keepdims=True) + 1e-05)
        * norm_gain
    ).astype(bf16)
    spread[3], normed = tie(spread[3], normed)
    column = pl.pallas_call(
        column_kernel,
        out_shape=jax.ShapeDtypeStruct((8, 2, BLK, HD), bf16),
        in_specs=[SSPEC] + [VSPEC] * NY,
        out_specs=VSPEC,
        compiler_params=params(8),
        cost_estimate=cost(0.8),
        name="column",
    )(tab, *spread)
    key_rows = jnp.dot(normed, w_key, preferred_element_type=f32).astype(bf16)
    value_rows = jnp.dot(normed, w_value, preferred_element_type=f32).astype(bf16)
    seqs = lax.axis_size("seq")
    route = [(i, (i + 1) % seqs) for i in range(seqs)]
    ring = [column] + [None] * 7
    ring[1], ring[7] = shift_z(column, 1), shift_z(column, -1)
    ring[1], key_rows, value_rows = tie(ring[1], key_rows, value_rows)
    ring[2], ring[6] = shift_z(ring[1], 1), shift_z(ring[7], -1)
    before_keys, before_values = lax.ppermute((key_rows, value_rows), "seq", route)
    queries = jnp.dot(normed, w_query, preferred_element_type=f32).astype(bf16)
    ring[2], queries = tie(ring[2], queries)
    ring[3], ring[5] = shift_z(ring[2], 1), shift_z(ring[6], -1)
    state_shape = [jax.ShapeDtypeStruct((GROUP, rows, HD), f32)] * 3
    state = pl.pallas_call(
        near_kernel,
        out_shape=state_shape,
        in_specs=[SSPEC] * 2 + [VSPEC] * 5,
        out_specs=[VSPEC] * 3,
        compiler_params=params(24),
        cost_estimate=cost(2.2),
        name="near",
    )(slash_offsets, slash_count, queries, before_keys, before_values, key_rows, value_rows)
    ring[4] = shift_z(ring[3], 1)
    ring[4], *state = tie(ring[4], *state)
    half = jax.ShapeDtypeStruct((2, 8 * BLK, HD), bf16)
    own = pl.pallas_call(
        row_kernel,
        out_shape=[half] * 2,
        in_specs=[SSPEC] + [VSPEC] * NZ,
        out_specs=[VSPEC] * 2,
        compiler_params=params(16),
        cost_estimate=cost(1.3),
        name="row",
    )(tab, *ring)
    lo1, hi3 = shift_y(own[0], 1), shift_y(own[1], -1)
    hi1, lo3 = shift_y(own[1], 1), shift_y(own[0], -1)
    lo2, hi2 = shift_y(lo1, 1), shift_y(hi3, -1)
    for shift, part in ((0, own), (1, (lo1, hi1)), (3, (lo3, hi3))):
        state = pl.pallas_call(
            functools.partial(far_kernel, shift),
            out_shape=state_shape,
            in_specs=[SSPEC] + [VSPEC] * 6,
            out_specs=[VSPEC] * 3,
            compiler_params=params(24),
            cost_estimate=cost(2.5),
            name="far",
        )(tab, queries, *part, *state)
    attended = pl.pallas_call(
        functools.partial(last_kernel, 2),
        out_shape=jax.ShapeDtypeStruct((rows, GROUP * HD), bf16),
        in_specs=[SSPEC] + [VSPEC] * 6,
        out_specs=VSPEC,
        compiler_params=params(24),
        cost_estimate=cost(2.5),
        name="last",
    )(tab, queries, lo2, hi2, *state)

    heads = lax.axis_index("heads")
    x, core = heads // 2, lax.rem(heads, 2)
    depth = GROUP * HD
    order = (x + jnp.arange(NX, dtype=jnp.int32)) & 3
    away_cols, home_cols = order * 2 + 1 - core, order * 2 + core
    att_spec = pl.BlockSpec((rows, depth), lambda i, cols: (0, 0))
    pieces = (0, 1, 3)

    def pick_piece(i, seq):
        return seq[0] if len(seq) == 1 else jnp.where(i == 2, seq[-1], i)

    def w_spec(seq):
        return pl.BlockSpec((depth, depth), lambda i, cols: (0, cols[pick_piece(i, seq)]))

    def piece_spec():
        return pl.BlockSpec((1, rows, depth), lambda i, cols: (i, 0, 0))

    def away(seq):
        return pl.pallas_call(
            away_kernel,
            out_shape=jax.ShapeDtypeStruct((len(seq), rows, depth), bf16),
            grid_spec=pltpu.PrefetchScalarGridSpec(
                num_scalar_prefetch=1,
                grid=(len(seq),),
                in_specs=[att_spec, w_spec(seq)],
                out_specs=piece_spec(),
            ),
            compiler_params=params(16),
            cost_estimate=cost(0.5 * len(seq)),
            name="away",
        )(away_cols, attended, w_out)

    recv_two = swap_core(away((2,)))
    recv = swap_core(away(pieces))
    upper, lower = pl.pallas_call(
        halves_kernel,
        out_shape=[jax.ShapeDtypeStruct((rows // 2, depth), bf16)] * 2,
        grid_spec=pltpu.PrefetchScalarGridSpec(
            num_scalar_prefetch=1,
            grid=(1,),
            in_specs=[att_spec, w_spec((2,)), piece_spec()],
            out_specs=[pl.BlockSpec((rows // 2, depth), lambda i, cols: (0, 0))] * 2,
        ),
        compiler_params=params(16),
        cost_estimate=cost(0.8),
        name="halves",
    )(home_cols, attended, w_out, recv_two)
    upper, lower = shift_x(upper, 1), shift_x(lower, -1)
    home = pl.pallas_call(
        home_kernel,
        out_shape=jax.ShapeDtypeStruct((3, rows, depth), f32),
        grid_spec=pltpu.PrefetchScalarGridSpec(
            num_scalar_prefetch=1,
            grid=(3,),
            in_specs=[att_spec, w_spec(pieces), piece_spec()],
            out_specs=piece_spec(),
        ),
        compiler_params=params(16),
        cost_estimate=cost(1.5),
        name="home",
    )(home_cols, attended, w_out, recv)
    right, left = pl.pallas_call(
        pass_kernel,
        out_shape=[jax.ShapeDtypeStruct((rows, depth), bf16)] * 2,
        in_specs=[VSPEC] * 3,
        out_specs=[VSPEC] * 2,
        compiler_params=params(16),
        cost_estimate=cost(0.6),
        name="pass",
    )(home, upper, lower)
    return pl.pallas_call(
        final_kernel,
        out_shape=jax.ShapeDtypeStruct((rows, depth), bf16),
        in_specs=[VSPEC] * 3,
        out_specs=VSPEC,
        compiler_params=params(16),
        cost_estimate=cost(0.6),
        name="final",
    )(home, shift_x(right, 1), shift_x(left, -1))


def solution(mesh):
    return jax.shard_map(
        local,
        mesh=mesh,
        in_specs=(
            P("seq", None),
            P(),
            P(None, "heads"),
            P(None, "heads"),
            P(None, "heads"),
            P("heads", None),
            P("heads", "seq", None),
            P("heads", "seq", None),
            P("heads", None),
            P("heads"),
            P("heads", None),
            P("heads"),
        ),
        out_specs=P("seq", "heads"),
        check_vma=False,
    )
```

```python
import functools
import math

import jax
import jax.numpy as jnp
from jax import lax
from jax.experimental import pallas as pl
from jax.experimental.pallas import tpu as pltpu
from jax.sharding import PartitionSpec as P

BLK = 64
HD = 128
GROUP = 4
NY = 4
NZ = 8
NX = 4
VMEM = pltpu.VMEM
VSPEC = pl.BlockSpec(memory_space=pltpu.VMEM)
SSPEC = pl.BlockSpec(memory_space=pltpu.SMEM)
SCALE2 = math.log2(math.e) / math.sqrt(HD)
NEG = -jnp.inf
LOW = -1e30
CHUNK = 4


def params(mib):
    return pltpu.CompilerParams(vmem_limit_bytes=mib << 20)


def cost(us):
    return pl.CostEstimate(flops=int(us * 1e9), bytes_accessed=0, transcendentals=0)


def tie(*values):
    return lax.optimization_barrier(values)


def shift_y(block, d):
    return lax.ppermute(
        block, "seq", [(y * NZ + z, (y + d) % NY * NZ + z) for y in range(NY) for z in range(NZ)]
    )


def shift_z(block, d):
    return lax.ppermute(
        block, "seq", [(y * NZ + z, y * NZ + (z + d) % NZ) for y in range(NY) for z in range(NZ)]
    )


def shift_x(block, d):
    return lax.ppermute(
        block, "heads", [(2 * x + c, 2 * ((x + d) % NX) + c) for x in range(NX) for c in range(2)]
    )


def swap_core(block):
    return lax.ppermute(block, "heads", [(i, i ^ 1) for i in range(2 * NX)])


def position():
    me = lax.axis_index("seq")
    return me // NZ, lax.rem(me, NZ)


def at(tab, group):
    return tab[64 + group]


def held(tab, d):
    y, z = position()
    group = ((z - d) & 7) * NY + y
    return at(tab, group), at(tab, group + 1) - at(tab, group)


def pick_kernel(tab, ck, cv, out):
    start, size = held(tab, 0)
    for i in range(8):
        entry = tab[jnp.minimum(start + i, 63)]
        row = pl.multiple_of(jnp.where(i < size, entry & 15, 0) * BLK, BLK)
        out[i, 0] = ck[0, pl.ds(row, BLK), :]
        out[i, 1] = cv[0, pl.ds(row, BLK), :]


def near_kernel(offs, cnt, q, kp, vp, k, v, m_out, l_out, acc_out):
    me = lax.axis_index("seq")
    rows = k.shape[0]
    keys = jnp.concatenate([kp[...], k[...]], axis=0)
    values = jnp.concatenate([vp[...], v[...]], axis=0)
    t = lax.broadcasted_iota(jnp.int32, (rows, 2 * rows), 0)
    u = lax.broadcasted_iota(jnp.int32, (rows, 2 * rows), 1) - rows
    gap = (t >> 6) - (u >> 6)
    hit = (gap == 0) & (u <= t)
    for e in range(4):
        off = jnp.where((e < cnt[0]) & (offs[0, e] >= 0), offs[0, e], -100)
        hit = hit | (gap == off)
    hit = hit & (u >= jnp.where(me > 0, -rows, 0))
    for h in range(GROUP):
        s = lax.dot_general(
            q[:, h * HD : (h + 1) * HD],
            keys,
            (((1,), (1,)), ((), ())),
            preferred_element_type=jnp.float32,
        )
        s = jnp.where(hit, s, NEG)
        top = jnp.max(s, axis=1, keepdims=True)
        p = jnp.exp2((s - top) * SCALE2)
        m_out[h] = jnp.broadcast_to(top, (rows, HD))
        l_out[h] = jnp.broadcast_to(jnp.sum(p, axis=1, keepdims=True), (rows, HD))
        acc_out[h] = jnp.dot(p.astype(jnp.bfloat16), values, preferred_element_type=jnp.float32)


def update(q, k, v, live, old, total, acc):
    s = lax.dot_general(q, k, (((1,), (1,)), ((), ())), preferred_element_type=jnp.float32)
    key = lax.broadcasted_iota(jnp.int32, s.shape, 1)
    s = jnp.where(key < live, s, NEG)
    top = jnp.maximum(old, jnp.max(s, axis=1, keepdims=True))
    factor = jnp.exp2((old - top) * SCALE2)
    p = jnp.exp2((s - top) * SCALE2)
    total = total * factor + jnp.sum(p, axis=1, keepdims=True)
    acc = acc * factor + jnp.dot(p.astype(jnp.bfloat16), v, preferred_element_type=jnp.float32)
    return top, total, acc


def gather_live(tab, shifts, kvs, kbuf, vbuf):
    base = 0
    for d, kv in zip(shifts, kvs):
        _, size = held(tab, d)
        for i in range(8):

            @pl.when(i < size)
            def _():
                row = pl.multiple_of((base + i) * BLK, BLK)
                kbuf[pl.ds(row, BLK), :] = kv[i, 0]
                vbuf[pl.ds(row, BLK), :] = kv[i, 1]

        base = base + size
    for i in range(CHUNK - 1):
        row = pl.multiple_of((base + i) * BLK, BLK)
        kbuf[pl.ds(row, BLK), :] = jnp.zeros((BLK, HD), kbuf.dtype)
        vbuf[pl.ds(row, BLK), :] = jnp.zeros((BLK, HD), vbuf.dtype)
    return base


def attend(tab, shifts, qs, kvs, states, kbuf, vbuf):
    slots = gather_live(tab, shifts, kvs, kbuf, vbuf)
    width = CHUNK * BLK

    def step(c, carry):
        row = pl.multiple_of(c * width, width)
        k, v = kbuf[pl.ds(row, width), :], vbuf[pl.ds(row, width), :]
        live = slots * BLK - row
        for g, q in enumerate(qs):
            m, l, acc = states[min(g, 1)]
            for h in range(GROUP):
                i = h if g == 0 else (g - 1) * GROUP + h
                top, total, sums = update(
                    q[:, h * HD : (h + 1) * HD], k, v, live, m[i][:, :1], l[i][:, :1], acc[i]
                )
                m[i] = jnp.broadcast_to(top, m.shape[1:])
                l[i] = jnp.broadcast_to(total, l.shape[1:])
                acc[i] = sums
        return carry

    lax.fori_loop(0, (slots + CHUNK - 1) // CHUNK, step, 0)


def first_kernel(shifts, tab, q0, q1, q2, q3, *refs):
    n = len(shifts)
    kvs, near, own, far = refs[:n], refs[n : n + 3], refs[n + 3 : n + 6], refs[n + 6 : n + 9]
    for a, b in zip(near, own):
        b[...] = a[...]
    far[0][...] = jnp.full(far[0].shape, LOW, jnp.float32)
    far[1][...] = jnp.zeros(far[1].shape, jnp.float32)
    far[2][...] = jnp.zeros(far[2].shape, jnp.float32)
    attend(tab, shifts, (q0, q1, q2, q3), kvs, (own, far), *refs[n + 9 :])


def more_kernel(shifts, tab, q0, q1, q2, q3, *refs):
    n = len(shifts)
    kvs, old = refs[:n], refs[n : n + 6]
    new = refs[n + 6 : n + 12]
    for a, b in zip(old, new):
        b[...] = a[...]
    attend(tab, shifts, (q0, q1, q2, q3), kvs, (new[:3], new[3:]), *refs[n + 12 :])


def sized(size, run):
    for low, high in ((-1, 2), (2, 4), (4, 8)):

        @pl.when((size > low) & (size <= high))
        def _():
            run(high)


def whole_source(kv, slots):
    k = kv[:slots, 0].reshape(slots * BLK, HD)
    return k, kv[:slots, 1].reshape(slots * BLK, HD)


def back_kernel(shift, tab, q1, q2, q3, kv, m, l, acc, o1, o2, o3):
    _, size = held(tab, shift)
    rows = q1.shape[0]

    def run(slots):
        k, v = whole_source(kv, slots)
        lane = lax.broadcasted_iota(jnp.int32, (rows, HD), 1)
        for g, (q, out) in enumerate(((q1, o1), (q2, o2), (q3, o3))):
            stats = jnp.zeros((rows, HD), jnp.float32)
            for h in range(GROUP):
                i = g * GROUP + h
                top, total, sums = update(
                    q[:, h * HD : (h + 1) * HD],
                    k,
                    v,
                    size * BLK,
                    m[i][:, :1],
                    l[i][:, :1],
                    acc[i],
                )
                some = total > 0
                safe = jnp.where(some, total, 1.0)
                out[:, h * HD : (h + 1) * HD] = (sums / safe).astype(out.dtype)
                log = jnp.where(some, top * SCALE2 + jnp.log2(safe), LOW)
                for term in range(3):
                    part = log.astype(jnp.bfloat16).astype(jnp.float32)
                    stats = jnp.where(lane == 3 * h + term, part, stats)
                    log = log - part
            out[:, GROUP * HD :] = stats.astype(out.dtype)

    sized(size, run)


def own_kernel(shift, tab, q, kv, m, l, acc, m_out, l_out, acc_out):
    _, size = held(tab, shift)

    def run(slots):
        k, v = whole_source(kv, slots)
        for h in range(GROUP):
            top, total, sums = update(
                q[:, h * HD : (h + 1) * HD], k, v, size * BLK, m[h][:, :1], l[h][:, :1], acc[h]
            )
            m_out[h] = jnp.broadcast_to(top, m_out.shape[1:])
            l_out[h] = jnp.broadcast_to(total, l_out.shape[1:])
            acc_out[h] = sums

    sized(size, run)


def merge_kernel(m, l, acc, r1, r2, r3, att):
    for h in range(GROUP):
        own_log = m[h][:, :1] * SCALE2
        logs = []
        for r in (r1, r2, r3):
            stats = r[:, GROUP * HD :].astype(jnp.float32)
            i = 3 * h
            logs.append(stats[:, i : i + 1] + stats[:, i + 1 : i + 2] + stats[:, i + 2 : i + 3])
        top = jnp.maximum(jnp.maximum(own_log, logs[0]), jnp.maximum(logs[1], logs[2]))
        factor = jnp.exp2(own_log - top)
        total = l[h][:, :1] * factor
        sums = acc[h] * factor
        for r, log in zip((r1, r2, r3), logs):
            weight = jnp.exp2(log - top)
            total = total + weight
            sums = sums + weight * r[:, h * HD : (h + 1) * HD].astype(jnp.float32)
        att[:, h * HD : (h + 1) * HD] = (sums / total).astype(att.dtype)


def away_kernel(cols, att, w, out):
    out[0] = jnp.dot(att[...], w[...], preferred_element_type=jnp.float32).astype(out.dtype)


def home_kernel(cols, att, w, recv, out):
    mine = jnp.dot(att[...], w[...], preferred_element_type=jnp.float32)
    out[0] = mine + recv[0].astype(jnp.float32)


def halves_kernel(cols, att, w, recv, a, b):
    mine = jnp.dot(att[...], w[...], preferred_element_type=jnp.float32)
    total = (mine + recv[0].astype(jnp.float32)).astype(a.dtype)
    half = a.shape[0]
    a[...] = total[:half]
    b[...] = total[half:]


def pass_kernel(home, a, b, right, left):
    half = a.shape[0]
    right[:half] = (home[1, :half] + a[...].astype(jnp.float32)).astype(right.dtype)
    right[half:] = home[1, half:].astype(right.dtype)
    left[:half] = home[2, :half].astype(left.dtype)
    left[half:] = (home[2, half:] + b[...].astype(jnp.float32)).astype(left.dtype)


def final_kernel(home, a, b, out):
    total = home[0] + a[...].astype(jnp.float32) + b[...].astype(jnp.float32)
    out[...] = total.astype(out.dtype)


def local(
    tokens,
    norm_gain,
    w_query,
    w_key,
    w_value,
    w_out,
    cache_keys,
    cache_values,
    vert_blocks,
    vert_count,
    slash_offsets,
    slash_count,
):
    rows = tokens.shape[0]
    bf16 = jnp.bfloat16
    f32 = jnp.float32
    blocks = vert_blocks[0]
    index = jnp.arange(128, dtype=jnp.int32)
    entry = index[:64]
    key = jnp.where(
        entry < vert_count[0],
        (((blocks >> 4) & 7) << 6) | ((blocks >> 7) << 4) | (blocks & 15),
        4096 + entry,
    )
    edges = jnp.concatenate([key, entry * 16])
    below = jnp.sum((key[None, :] < edges[:, None]).astype(jnp.int32), axis=1)
    ranked = jnp.sum(jnp.where(below[None, :64] == index[:, None], key[None, :], 0), axis=1)
    tab = jnp.where(index < 64, ranked, below)

    picked = pl.pallas_call(
        pick_kernel,
        out_shape=jax.ShapeDtypeStruct((8, 2, BLK, HD), bf16),
        in_specs=[SSPEC, VSPEC, VSPEC],
        out_specs=VSPEC,
        compiler_params=params(8),
        cost_estimate=cost(0.7),
        name="pick",
    )(tab, cache_keys, cache_values)
    ring = [picked] + [None] * 7
    ring[1], ring[7] = shift_z(picked, 1), shift_z(picked, -1)
    activation = tokens.astype(f32)
    normed = (
        activation
        * lax.rsqrt(jnp.mean(activation * activation, axis=-1, keepdims=True) + 1e-05)
        * norm_gain
    ).astype(bf16)
    queries = jnp.dot(normed, w_query, preferred_element_type=f32).astype(bf16)
    ring[1], queries = tie(ring[1], queries)
    column_queries = [queries] + [shift_y(queries, d) for d in (1, 2, 3)]
    key_rows = jnp.dot(normed, w_key, preferred_element_type=f32).astype(bf16)
    value_rows = jnp.dot(normed, w_value, preferred_element_type=f32).astype(bf16)
    seqs = lax.axis_size("seq")
    route = [(i, (i + 1) % seqs) for i in range(seqs)]
    before_keys, before_values = lax.ppermute((key_rows, value_rows), "seq", route)
    ring[2], ring[6] = shift_z(ring[1], 1), shift_z(ring[7], -1)
    near_shape = [jax.ShapeDtypeStruct((GROUP, rows, HD), f32)] * 3
    near = pl.pallas_call(
        near_kernel,
        out_shape=near_shape,
        in_specs=[SSPEC] * 2 + [VSPEC] * 5,
        out_specs=[VSPEC] * 3,
        compiler_params=params(24),
        cost_estimate=cost(2.2),
        name="near",
    )(slash_offsets, slash_count, queries, before_keys, before_values, key_rows, value_rows)
    ring[2], *near = tie(ring[2], *near)
    ring[3], ring[5] = shift_z(ring[2], 1), shift_z(ring[6], -1)
    far_shape = [jax.ShapeDtypeStruct((3 * GROUP, rows, HD), f32)] * 3

    def buffers(sources):
        return [VMEM(((8 * sources + CHUNK - 1) * BLK, HD), bf16)] * 2

    shifts = (0, 1, 7, 2, 6)
    state = pl.pallas_call(
        functools.partial(first_kernel, shifts),
        out_shape=near_shape + far_shape,
        in_specs=[SSPEC] + [VSPEC] * 12,
        out_specs=[VSPEC] * 6,
        scratch_shapes=buffers(5),
        input_output_aliases={10 + i: i for i in range(3)},
        compiler_params=params(32),
        cost_estimate=cost(5),
        name="first",
    )(tab, *column_queries, *[ring[d] for d in shifts], *near)
    ring[3], *state = tie(ring[3], *state)
    ring[4] = shift_z(ring[3], 1)
    shifts = (3, 5)
    state = pl.pallas_call(
        functools.partial(more_kernel, shifts),
        out_shape=near_shape + far_shape,
        in_specs=[SSPEC] + [VSPEC] * 12,
        out_specs=[VSPEC] * 6,
        scratch_shapes=buffers(2),
        input_output_aliases={7 + i: i for i in range(6)},
        compiler_params=params(32),
        cost_estimate=cost(3),
        name="more",
    )(tab, *column_queries, *[ring[d] for d in shifts], *state)
    ring[4], *state = tie(ring[4], *state)
    partial_shape = jax.ShapeDtypeStruct((rows, (GROUP + 1) * HD), bf16)
    partials = pl.pallas_call(
        functools.partial(back_kernel, 4),
        out_shape=[partial_shape] * 3,
        in_specs=[SSPEC] + [VSPEC] * 7,
        out_specs=[VSPEC] * 3,
        compiler_params=params(32),
        cost_estimate=cost(2),
        name="back",
    )(tab, *column_queries[1:], ring[4], *state[3:])
    returned = [shift_y(partials[d - 1], -d) for d in (2, 1, 3)]
    own = pl.pallas_call(
        functools.partial(own_kernel, 4),
        out_shape=near_shape,
        in_specs=[SSPEC] + [VSPEC] * 5,
        out_specs=[VSPEC] * 3,
        compiler_params=params(24),
        cost_estimate=cost(1),
        name="own",
    )(tab, queries, ring[4], *state[:3])
    attended = pl.pallas_call(
        merge_kernel,
        out_shape=jax.ShapeDtypeStruct((rows, GROUP * HD), bf16),
        in_specs=[VSPEC] * 6,
        out_specs=VSPEC,
        compiler_params=params(24),
        cost_estimate=cost(1),
        name="merge",
    )(*own, *returned)

    heads = lax.axis_index("heads")
    x, core = heads // 2, lax.rem(heads, 2)
    depth = GROUP * HD
    order = (x + jnp.arange(NX, dtype=jnp.int32)) & 3
    away_cols, home_cols = order * 2 + 1 - core, order * 2 + core
    att_spec = pl.BlockSpec((rows, depth), lambda i, cols: (0, 0))
    pieces = (0, 1, 3)

    def pick_piece(i, seq):
        return seq[0] if len(seq) == 1 else jnp.where(i == 2, seq[-1], i)

    def w_spec(seq):
        return pl.BlockSpec((depth, depth), lambda i, cols: (0, cols[pick_piece(i, seq)]))

    def piece_spec():
        return pl.BlockSpec((1, rows, depth), lambda i, cols: (i, 0, 0))

    def away(seq, attended):
        return pl.pallas_call(
            away_kernel,
            out_shape=jax.ShapeDtypeStruct((len(seq), rows, depth), bf16),
            grid_spec=pltpu.PrefetchScalarGridSpec(
                num_scalar_prefetch=1,
                grid=(len(seq),),
                in_specs=[att_spec, w_spec(seq)],
                out_specs=piece_spec(),
            ),
            compiler_params=params(16),
            cost_estimate=cost(0.5 * len(seq)),
            name="away",
        )(away_cols, attended, w_out)

    away_two, attended = tie(away((2,), attended), attended)
    recv_two = swap_core(away_two)
    recv = swap_core(away(pieces, attended))
    upper, lower = pl.pallas_call(
        halves_kernel,
        out_shape=[jax.ShapeDtypeStruct((rows // 2, depth), bf16)] * 2,
        grid_spec=pltpu.PrefetchScalarGridSpec(
            num_scalar_prefetch=1,
            grid=(1,),
            in_specs=[att_spec, w_spec((2,)), piece_spec()],
            out_specs=[pl.BlockSpec((rows // 2, depth), lambda i, cols: (0, 0))] * 2,
        ),
        compiler_params=params(16),
        cost_estimate=cost(0.8),
        name="halves",
    )(home_cols, attended, w_out, recv_two)
    upper, lower = shift_x(upper, 1), shift_x(lower, -1)
    home = pl.pallas_call(
        home_kernel,
        out_shape=jax.ShapeDtypeStruct((3, rows, depth), f32),
        grid_spec=pltpu.PrefetchScalarGridSpec(
            num_scalar_prefetch=1,
            grid=(3,),
            in_specs=[att_spec, w_spec(pieces), piece_spec()],
            out_specs=piece_spec(),
        ),
        compiler_params=params(16),
        cost_estimate=cost(1.5),
        name="home",
    )(home_cols, attended, w_out, recv)
    right, left = pl.pallas_call(
        pass_kernel,
        out_shape=[jax.ShapeDtypeStruct((rows, depth), bf16)] * 2,
        in_specs=[VSPEC] * 3,
        out_specs=[VSPEC] * 2,
        compiler_params=params(16),
        cost_estimate=cost(0.6),
        name="pass",
    )(home, upper, lower)
    return pl.pallas_call(
        final_kernel,
        out_shape=jax.ShapeDtypeStruct((rows, depth), bf16),
        in_specs=[VSPEC] * 3,
        out_specs=VSPEC,
        compiler_params=params(16),
        cost_estimate=cost(0.6),
        name="final",
    )(home, shift_x(right, 1), shift_x(left, -1))


def solution(mesh):
    return jax.shard_map(
        local,
        mesh=mesh,
        in_specs=(
            P("seq", None),
            P(),
            P(None, "heads"),
            P(None, "heads"),
            P(None, "heads"),
            P("heads", None),
            P("heads", "seq", None),
            P("heads", "seq", None),
            P("heads", None),
            P("heads"),
            P("heads", None),
            P("heads"),
        ),
        out_specs=P("seq", "heads"),
        check_vma=False,
    )
```

```python
import functools
import math

import jax
import jax.numpy as jnp
from jax import lax
from jax.experimental import pallas as pl
from jax.experimental.pallas import tpu as pltpu
from jax.sharding import PartitionSpec as P

BLK = 64
HD = 128
GROUP = 4
NY = 4
NZ = 8
NX = 4
VMEM = pltpu.VMEM
VSPEC = pl.BlockSpec(memory_space=pltpu.VMEM)
SSPEC = pl.BlockSpec(memory_space=pltpu.SMEM)
SCALE2 = math.log2(math.e) / math.sqrt(HD)
NEG = -jnp.inf
LOW = -1e30
CHUNK = 4


def params(mib):
    return pltpu.CompilerParams(vmem_limit_bytes=mib << 20)


def cost(us):
    return pl.CostEstimate(flops=int(us * 1e9), bytes_accessed=0, transcendentals=0)


def tie(*values):
    return lax.optimization_barrier(values)


def shift_y(block, d):
    return lax.ppermute(
        block, "seq", [(y * NZ + z, (y + d) % NY * NZ + z) for y in range(NY) for z in range(NZ)]
    )


def shift_z(block, d):
    return lax.ppermute(
        block, "seq", [(y * NZ + z, y * NZ + (z + d) % NZ) for y in range(NY) for z in range(NZ)]
    )


def shift_x(block, d):
    return lax.ppermute(
        block, "heads", [(2 * x + c, 2 * ((x + d) % NX) + c) for x in range(NX) for c in range(2)]
    )


def swap_core(block):
    return lax.ppermute(block, "heads", [(i, i ^ 1) for i in range(2 * NX)])


def position():
    me = lax.axis_index("seq")
    return me // NZ, lax.rem(me, NZ)


def at(tab, group):
    return tab[64 + group]


def held(tab, d):
    y, z = position()
    group = ((z - d) & 7) * NY + y
    return at(tab, group), at(tab, group + 1) - at(tab, group)


def pick_kernel(tab, ck, cv, out):
    start, size = held(tab, 0)
    for i in range(8):
        entry = tab[jnp.minimum(start + i, 63)]
        row = pl.multiple_of(jnp.where(i < size, entry & 15, 0) * BLK, BLK)
        out[i, 0] = ck[0, pl.ds(row, BLK), :]
        out[i, 1] = cv[0, pl.ds(row, BLK), :]


def near_kernel(offs, cnt, q, kp, vp, k, v, m_out, l_out, acc_out):
    me = lax.axis_index("seq")
    rows = k.shape[0]
    keys = jnp.concatenate([kp[...], k[...]], axis=0)
    values = jnp.concatenate([vp[...], v[...]], axis=0)
    t = lax.broadcasted_iota(jnp.int32, (rows, 2 * rows), 0)
    u = lax.broadcasted_iota(jnp.int32, (rows, 2 * rows), 1) - rows
    gap = (t >> 6) - (u >> 6)
    hit = (gap == 0) & (u <= t)
    for e in range(4):
        off = jnp.where((e < cnt[0]) & (offs[0, e] >= 0), offs[0, e], -100)
        hit = hit | (gap == off)
    hit = hit & (u >= jnp.where(me > 0, -rows, 0))
    for h in range(GROUP):
        s = lax.dot_general(
            q[:, h * HD : (h + 1) * HD],
            keys,
            (((1,), (1,)), ((), ())),
            preferred_element_type=jnp.float32,
        )
        s = jnp.where(hit, s, NEG)
        top = jnp.broadcast_to(jnp.max(s, axis=1, keepdims=True), (rows, HD))
        p = jnp.exp2((s - across(top, 2 * rows)) * SCALE2)
        m_out[h] = top
        l_out[h] = lane_sums(p)
        acc_out[h] = jnp.dot(p.astype(jnp.bfloat16), values, preferred_element_type=jnp.float32)


def across(x, width):
    return jnp.concatenate([x] * (width // HD), axis=1)


def lane_sums(p):
    total = p[:, :HD]
    for i in range(HD, p.shape[1], HD):
        total = total + p[:, i : i + HD]
    return total


def scores_of(q, h, k):
    return lax.dot_general(
        q[:, h * HD : (h + 1) * HD], k, (((1,), (1,)), ((), ())), preferred_element_type=jnp.float32
    )


def update(s, v, live, old, total, acc):
    key = lax.broadcasted_iota(jnp.int32, s.shape, 1)
    s = jnp.where(key < live, s, NEG)
    top = jnp.maximum(old, jnp.broadcast_to(jnp.max(s, axis=1, keepdims=True), old.shape))
    factor = jnp.exp2((old - top) * SCALE2)
    p = jnp.exp2((s - across(top, s.shape[1])) * SCALE2)
    total = total * factor + lane_sums(p)
    acc = acc * factor + jnp.dot(p.astype(jnp.bfloat16), v, preferred_element_type=jnp.float32)
    return top, total, acc


def ahead(items, k):
    following = scores_of(items[0][1], items[0][2], k)
    for i, (g, _, h) in enumerate(items):
        current = following
        if i + 1 < len(items):
            following = scores_of(items[i + 1][1], items[i + 1][2], k)
        yield g, h, current


def row_sum(total):
    return jnp.broadcast_to(jnp.sum(total, axis=1, keepdims=True), total.shape)


def gather_live(tab, shifts, kvs, kbuf, vbuf):
    base = 0
    for d, kv in zip(shifts, kvs):
        _, size = held(tab, d)
        for i in range(8):

            @pl.when(i < size)
            def _():
                row = pl.multiple_of((base + i) * BLK, BLK)
                kbuf[pl.ds(row, BLK), :] = kv[i, 0]
                vbuf[pl.ds(row, BLK), :] = kv[i, 1]

        base = base + size
    for i in range(CHUNK - 1):
        row = pl.multiple_of((base + i) * BLK, BLK)
        kbuf[pl.ds(row, BLK), :] = jnp.zeros((BLK, HD), kbuf.dtype)
        vbuf[pl.ds(row, BLK), :] = jnp.zeros((BLK, HD), vbuf.dtype)
    return base


def attend(tab, shifts, qs, kvs, states, kbuf, vbuf):
    slots = gather_live(tab, shifts, kvs, kbuf, vbuf)
    width = CHUNK * BLK

    def step(c, carry):
        row = pl.multiple_of(c * width, width)
        k, v = kbuf[pl.ds(row, width), :], vbuf[pl.ds(row, width), :]
        live = slots * BLK - row
        items = [(g, q, h) for g, q in enumerate(qs) for h in range(GROUP)]
        for g, h, s in ahead(items, k):
            m, l, acc = states[min(g, 1)]
            i = h if g == 0 else (g - 1) * GROUP + h
            m[i], l[i], acc[i] = update(s, v, live, m[i], l[i], acc[i])
        return carry

    lax.fori_loop(0, (slots + CHUNK - 1) // CHUNK, step, 0)


def first_kernel(shifts, tab, q0, q1, q2, q3, *refs):
    n = len(shifts)
    kvs, near, own, far = refs[:n], refs[n : n + 3], refs[n + 3 : n + 6], refs[n + 6 : n + 9]
    for a, b in zip(near, own):
        b[...] = a[...]
    far[0][...] = jnp.full(far[0].shape, LOW, jnp.float32)
    far[1][...] = jnp.zeros(far[1].shape, jnp.float32)
    far[2][...] = jnp.zeros(far[2].shape, jnp.float32)
    attend(tab, shifts, (q0, q1, q2, q3), kvs, (own, far), *refs[n + 9 :])


def more_kernel(shifts, tab, q0, q1, q2, q3, *refs):
    n = len(shifts)
    kvs, old = refs[:n], refs[n : n + 6]
    new = refs[n + 6 : n + 12]
    for a, b in zip(old, new):
        b[...] = a[...]
    attend(tab, shifts, (q0, q1, q2, q3), kvs, (new[:3], new[3:]), *refs[n + 12 :])


def sized(size, run):
    for low, high in ((-1, 2), (2, 4), (4, 8)):

        @pl.when((size > low) & (size <= high))
        def _():
            run(high)


def whole_source(kv, slots):
    k = kv[:slots, 0].reshape(slots * BLK, HD)
    return k, kv[:slots, 1].reshape(slots * BLK, HD)


def back_kernel(shift, tab, q1, q2, q3, kv, m, l, acc, o1, o2, o3):
    _, size = held(tab, shift)
    rows = q1.shape[0]

    outs = (o1, o2, o3)

    def run(slots):
        k, v = whole_source(kv, slots)
        lane = lax.broadcasted_iota(jnp.int32, (rows, HD), 1)
        items = [(g, q, h) for g, q in enumerate((q1, q2, q3)) for h in range(GROUP)]
        for g, h, s in ahead(items, k):
            i = g * GROUP + h
            if h == 0:
                stats = jnp.zeros((rows, HD), jnp.float32)
            top, total, sums = update(s, v, size * BLK, m[i], l[i], acc[i])
            total = row_sum(total)
            some = total > 0
            safe = jnp.where(some, total, 1.0)
            outs[g][:, h * HD : (h + 1) * HD] = (sums / safe).astype(o1.dtype)
            log = jnp.where(some, top * SCALE2 + jnp.log2(safe), LOW)
            for term in range(3):
                part = log.astype(jnp.bfloat16).astype(jnp.float32)
                stats = jnp.where(lane == 3 * h + term, part, stats)
                log = log - part
            if h == GROUP - 1:
                outs[g][:, GROUP * HD :] = stats.astype(o1.dtype)

    sized(size, run)


def own_kernel(shift, tab, q, kv, m, l, acc, m_out, l_out, acc_out):
    _, size = held(tab, shift)

    def run(slots):
        k, v = whole_source(kv, slots)
        for _, h, s in ahead([(0, q, h) for h in range(GROUP)], k):
            m_out[h], l_out[h], acc_out[h] = update(s, v, size * BLK, m[h], l[h], acc[h])

    sized(size, run)


def merge_kernel(m, l, acc, r1, r2, r3, att):
    term = lax.broadcasted_iota(jnp.int32, (HD, HD), 0)
    for h in range(GROUP):
        own_log = m[h] * SCALE2
        pick = jnp.where((term >= 3 * h) & (term < 3 * h + 3), 1.0, 0.0).astype(jnp.bfloat16)
        logs = [
            jnp.dot(r[:, GROUP * HD :], pick, preferred_element_type=jnp.float32)
            for r in (r1, r2, r3)
        ]
        top = jnp.maximum(jnp.maximum(own_log, logs[0]), jnp.maximum(logs[1], logs[2]))
        factor = jnp.exp2(own_log - top)
        total = row_sum(l[h]) * factor
        sums = acc[h] * factor
        for r, log in zip((r1, r2, r3), logs):
            weight = jnp.exp2(log - top)
            total = total + weight
            sums = sums + weight * r[:, h * HD : (h + 1) * HD].astype(jnp.float32)
        att[:, h * HD : (h + 1) * HD] = (sums / total).astype(att.dtype)


def away_kernel(cols, att, w, out):
    out[0] = jnp.dot(att[...], w[...], preferred_element_type=jnp.float32).astype(out.dtype)


def home_kernel(cols, att, w, recv, out):
    mine = jnp.dot(att[...], w[...], preferred_element_type=jnp.float32)
    out[0] = mine + recv[0].astype(jnp.float32)


def halves_kernel(cols, att, w, recv, a, b):
    mine = jnp.dot(att[...], w[...], preferred_element_type=jnp.float32)
    total = (mine + recv[0].astype(jnp.float32)).astype(a.dtype)
    half = a.shape[0]
    a[...] = total[:half]
    b[...] = total[half:]


def pass_kernel(home, a, b, right, left):
    half = a.shape[0]
    right[:half] = (home[1, :half] + a[...].astype(jnp.float32)).astype(right.dtype)
    right[half:] = home[1, half:].astype(right.dtype)
    left[:half] = home[2, :half].astype(left.dtype)
    left[half:] = (home[2, half:] + b[...].astype(jnp.float32)).astype(left.dtype)


def final_kernel(home, a, b, out):
    total = home[0] + a[...].astype(jnp.float32) + b[...].astype(jnp.float32)
    out[...] = total.astype(out.dtype)


def local(
    tokens,
    norm_gain,
    w_query,
    w_key,
    w_value,
    w_out,
    cache_keys,
    cache_values,
    vert_blocks,
    vert_count,
    slash_offsets,
    slash_count,
):
    rows = tokens.shape[0]
    bf16 = jnp.bfloat16
    f32 = jnp.float32
    blocks = vert_blocks[0]
    index = jnp.arange(128, dtype=jnp.int32)
    entry = index[:64]
    key = jnp.where(
        entry < vert_count[0],
        (((blocks >> 4) & 7) << 6) | ((blocks >> 7) << 4) | (blocks & 15),
        4096 + entry,
    )
    edges = jnp.concatenate([key, entry * 16])
    below = jnp.sum((key[None, :] < edges[:, None]).astype(jnp.int32), axis=1)
    ranked = jnp.sum(jnp.where(below[None, :64] == index[:, None], key[None, :], 0), axis=1)
    tab = jnp.where(index < 64, ranked, below)

    picked = pl.pallas_call(
        pick_kernel,
        out_shape=jax.ShapeDtypeStruct((8, 2, BLK, HD), bf16),
        grid=(1,),
        in_specs=[SSPEC] + [pl.BlockSpec(cache_keys.shape, lambda i: (0, 0, 0))] * 2,
        out_specs=VSPEC,
        compiler_params=params(8),
        cost_estimate=cost(0.7),
        name="pick",
    )(tab, cache_keys, cache_values)
    ring = [picked] + [None] * 7
    ring[1], ring[7] = shift_z(picked, 1), shift_z(picked, -1)
    activation = tokens.astype(f32)
    normed = (
        activation
        * lax.rsqrt(jnp.mean(activation * activation, axis=-1, keepdims=True) + 1e-05)
        * norm_gain
    ).astype(bf16)
    queries = jnp.dot(normed, w_query, preferred_element_type=f32).astype(bf16)
    ring[1], queries = tie(ring[1], queries)
    column_queries = [queries] + [shift_y(queries, d) for d in (1, 2, 3)]
    key_rows = jnp.dot(normed, w_key, preferred_element_type=f32).astype(bf16)
    value_rows = jnp.dot(normed, w_value, preferred_element_type=f32).astype(bf16)
    seqs = lax.axis_size("seq")
    route = [(i, (i + 1) % seqs) for i in range(seqs)]
    before_keys, before_values = lax.ppermute((key_rows, value_rows), "seq", route)
    ring[2], ring[6] = shift_z(ring[1], 1), shift_z(ring[7], -1)
    near_shape = [jax.ShapeDtypeStruct((GROUP, rows, HD), f32)] * 3
    near = pl.pallas_call(
        near_kernel,
        out_shape=near_shape,
        in_specs=[SSPEC] * 2 + [VSPEC] * 5,
        out_specs=[VSPEC] * 3,
        compiler_params=params(16),
        cost_estimate=cost(2.2),
        name="near",
    )(slash_offsets, slash_count, queries, before_keys, before_values, key_rows, value_rows)
    ring[2], *near = tie(ring[2], *near)
    ring[3], ring[5] = shift_z(ring[2], 1), shift_z(ring[6], -1)
    far_shape = [jax.ShapeDtypeStruct((3 * GROUP, rows, HD), f32)] * 3

    def buffers(sources):
        return [VMEM(((8 * sources + CHUNK - 1) * BLK, HD), bf16)] * 2

    shifts = (0, 1, 7, 2, 6)
    state = pl.pallas_call(
        functools.partial(first_kernel, shifts),
        out_shape=near_shape + far_shape,
        in_specs=[SSPEC] + [VSPEC] * 12,
        out_specs=[VSPEC] * 6,
        scratch_shapes=buffers(5),
        input_output_aliases={10 + i: i for i in range(3)},
        compiler_params=params(20),
        cost_estimate=cost(5),
        name="first",
    )(tab, *column_queries, *[ring[d] for d in shifts], *near)
    ring[3], *state = tie(ring[3], *state)
    ring[4] = shift_z(ring[3], 1)
    shifts = (3, 5)
    state = pl.pallas_call(
        functools.partial(more_kernel, shifts),
        out_shape=near_shape + far_shape,
        in_specs=[SSPEC] + [VSPEC] * 12,
        out_specs=[VSPEC] * 6,
        scratch_shapes=buffers(2),
        input_output_aliases={7 + i: i for i in range(6)},
        compiler_params=params(20),
        cost_estimate=cost(3),
        name="more",
    )(tab, *column_queries, *[ring[d] for d in shifts], *state)
    ring[4], *state = tie(ring[4], *state)
    partial_shape = jax.ShapeDtypeStruct((rows, (GROUP + 1) * HD), bf16)
    partials = pl.pallas_call(
        functools.partial(back_kernel, 4),
        out_shape=[partial_shape] * 3,
        in_specs=[SSPEC] + [VSPEC] * 7,
        out_specs=[VSPEC] * 3,
        compiler_params=params(20),
        cost_estimate=cost(2),
        name="back",
    )(tab, *column_queries[1:], ring[4], *state[3:])
    returned = [shift_y(partials[d - 1], -d) for d in (2, 1, 3)]
    own = pl.pallas_call(
        functools.partial(own_kernel, 4),
        out_shape=near_shape,
        in_specs=[SSPEC] + [VSPEC] * 5,
        out_specs=[VSPEC] * 3,
        compiler_params=params(16),
        cost_estimate=cost(1),
        name="own",
    )(tab, queries, ring[4], *state[:3])
    attended = pl.pallas_call(
        merge_kernel,
        out_shape=jax.ShapeDtypeStruct((rows, GROUP * HD), bf16),
        in_specs=[VSPEC] * 6,
        out_specs=VSPEC,
        compiler_params=params(16),
        cost_estimate=cost(1),
        name="merge",
    )(*own, *returned)

    heads = lax.axis_index("heads")
    x, core = heads // 2, lax.rem(heads, 2)
    depth = GROUP * HD
    order = (x + jnp.arange(NX, dtype=jnp.int32)) & 3
    away_cols, home_cols = order * 2 + 1 - core, order * 2 + core
    att_spec = pl.BlockSpec((rows, depth), lambda i, cols: (0, 0))
    pieces = (0, 1, 3)

    def pick_piece(i, seq):
        return seq[0] if len(seq) == 1 else jnp.where(i == 2, seq[-1], i)

    def w_spec(seq):
        return pl.BlockSpec((depth, depth), lambda i, cols: (0, cols[pick_piece(i, seq)]))

    def piece_spec():
        return pl.BlockSpec((1, rows, depth), lambda i, cols: (i, 0, 0))

    def away(seq, attended):
        return pl.pallas_call(
            away_kernel,
            out_shape=jax.ShapeDtypeStruct((len(seq), rows, depth), bf16),
            grid_spec=pltpu.PrefetchScalarGridSpec(
                num_scalar_prefetch=1,
                grid=(len(seq),),
                in_specs=[att_spec, w_spec(seq)],
                out_specs=piece_spec(),
            ),
            compiler_params=params(16),
            cost_estimate=cost(0.5 * len(seq)),
            name="away",
        )(away_cols, attended, w_out)

    away_two, attended = tie(away((2,), attended), attended)
    recv_two = swap_core(away_two)
    recv = swap_core(away(pieces, attended))
    upper, lower = pl.pallas_call(
        halves_kernel,
        out_shape=[jax.ShapeDtypeStruct((rows // 2, depth), bf16)] * 2,
        grid_spec=pltpu.PrefetchScalarGridSpec(
            num_scalar_prefetch=1,
            grid=(1,),
            in_specs=[att_spec, w_spec((2,)), piece_spec()],
            out_specs=[pl.BlockSpec((rows // 2, depth), lambda i, cols: (0, 0))] * 2,
        ),
        compiler_params=params(16),
        cost_estimate=cost(0.8),
        name="halves",
    )(home_cols, attended, w_out, recv_two)
    upper, lower = shift_x(upper, 1), shift_x(lower, -1)
    home = pl.pallas_call(
        home_kernel,
        out_shape=jax.ShapeDtypeStruct((3, rows, depth), f32),
        grid_spec=pltpu.PrefetchScalarGridSpec(
            num_scalar_prefetch=1,
            grid=(3,),
            in_specs=[att_spec, w_spec(pieces), piece_spec()],
            out_specs=piece_spec(),
        ),
        compiler_params=params(16),
        cost_estimate=cost(1.5),
        name="home",
    )(home_cols, attended, w_out, recv)
    right, left = pl.pallas_call(
        pass_kernel,
        out_shape=[jax.ShapeDtypeStruct((rows, depth), bf16)] * 2,
        in_specs=[VSPEC] * 3,
        out_specs=[VSPEC] * 2,
        compiler_params=params(16),
        cost_estimate=cost(0.6),
        name="pass",
    )(home, upper, lower)
    return pl.pallas_call(
        final_kernel,
        out_shape=jax.ShapeDtypeStruct((rows, depth), bf16),
        in_specs=[VSPEC] * 3,
        out_specs=VSPEC,
        compiler_params=params(16),
        cost_estimate=cost(0.6),
        name="final",
    )(home, shift_x(right, 1), shift_x(left, -1))


def solution(mesh):
    return jax.shard_map(
        local,
        mesh=mesh,
        in_specs=(
            P("seq", None),
            P(),
            P(None, "heads"),
            P(None, "heads"),
            P(None, "heads"),
            P("heads", None),
            P("heads", "seq", None),
            P("heads", "seq", None),
            P("heads", None),
            P("heads"),
            P("heads", None),
            P("heads"),
        ),
        out_specs=P("seq", "heads"),
        check_vma=False,
    )
```

```python
import functools
import math

import jax
import jax.numpy as jnp
from jax import lax
from jax.experimental import pallas as pl
from jax.experimental.pallas import tpu as pltpu
from jax.sharding import PartitionSpec as P

BLK = 64
HD = 128
GROUP = 4
NY = 4
NZ = 8
NX = 4
VMEM = pltpu.VMEM
VSPEC = pl.BlockSpec(memory_space=pltpu.VMEM)
HSPEC = pl.BlockSpec(memory_space=pltpu.HBM)
SSPEC = pl.BlockSpec(memory_space=pltpu.SMEM)
SCALE2 = math.log2(math.e) / math.sqrt(HD)
NEG = -jnp.inf


def params(mib):
    return pltpu.CompilerParams(vmem_limit_bytes=mib << 20)


def cost(us):
    return pl.CostEstimate(flops=int(us * 1e9), bytes_accessed=0, transcendentals=0)


def tie(*values):
    return lax.optimization_barrier(values)


def shift_y(block, d):
    return lax.ppermute(
        block, "seq", [(y * NZ + z, (y + d) % NY * NZ + z) for y in range(NY) for z in range(NZ)]
    )


def shift_z(block, d):
    return lax.ppermute(
        block, "seq", [(y * NZ + z, y * NZ + (z + d) % NZ) for y in range(NY) for z in range(NZ)]
    )


def shift_x(block, d):
    return lax.ppermute(
        block, "heads", [(2 * x + c, 2 * ((x + d) % NX) + c) for x in range(NX) for c in range(2)]
    )


def swap_core(block):
    return lax.ppermute(block, "heads", [(i, i ^ 1) for i in range(2 * NX)])


def position():
    me = lax.axis_index("seq")
    return me // NZ, lax.rem(me, NZ)


def at(tab, group):
    return tab[64 + group]


def pick_kernel(tab, ck, cv, *refs):
    outs, sems = refs[:NY], refs[NY]
    y, z = position()
    group = z * NY + y
    start = at(tab, group)
    size = at(tab, group + 1) - start
    copies = []
    for dy in range(NY):
        for j in range(2):
            i = ((y + dy - start) & 3) + 4 * j
            entry = tab[jnp.minimum(start + i, 63)]
            row = pl.multiple_of(jnp.where(i < size, entry & 15, 0) * BLK, BLK)
            for k, cache in enumerate((ck, cv)):
                copies.append(
                    pltpu.make_async_copy(
                        cache.at[0, pl.ds(row, BLK)], outs[dy].at[j, k], sems.at[len(copies)]
                    )
                )
    for copy in copies:
        copy.start()
    for copy in copies:
        copy.wait()


def column_kernel(tab, r0, r1, r2, r3, out):
    y, z = position()
    recv = (r0, r1, r2, r3)
    start = at(tab, z * NY)
    size = at(tab, z * NY + NY) - start
    first = (y - start) & 3
    for i in range(8):
        off = first + 4 * i
        live = off < size
        r = jnp.minimum(start + off, 63)
        hy = (tab[r] >> 4) & 3
        j = jnp.where(live, (r - at(tab, z * NY + hy)) >> 2, 0)
        d = jnp.where(live, (y - hy) & 3, 0)
        for k in range(NY):

            @pl.when(d == k)
            def _():
                out[i] = recv[k][j]


def row_kernel(tab, *refs):
    y, z = position()
    recv, outs = refs[:NZ], refs[NZ:]
    for m in range(16):
        r = y + 4 * m
        live = r < at(tab, 32)
        zs = jnp.where(live, tab[r] >> 6, z)
        start = at(tab, zs * NY)
        first = (y - start) & 3
        i = jnp.where(live, (r - start - first) >> 2, 0)
        d = (z - zs) & 7
        out, place = outs[m // 8], m % 8 * BLK
        for k in range(NZ):

            @pl.when(d == k)
            def _():
                out[0, place : place + BLK] = recv[k][i, 0]
                out[1, place : place + BLK] = recv[k][i, 1]


def near_kernel(offs, cnt, q, kp, vp, k, v, m_out, l_out, acc_out):
    me = lax.axis_index("seq")
    rows = k.shape[0]
    keys = jnp.concatenate([kp[...], k[...]], axis=0)
    values = jnp.concatenate([vp[...], v[...]], axis=0)
    t = lax.broadcasted_iota(jnp.int32, (rows, 2 * rows), 0)
    u = lax.broadcasted_iota(jnp.int32, (rows, 2 * rows), 1) - rows
    gap = (t >> 6) - (u >> 6)
    hit = (gap == 0) & (u <= t)
    for e in range(4):
        off = jnp.where((e < cnt[0]) & (offs[0, e] >= 0), offs[0, e], -100)
        hit = hit | (gap == off)
    hit = hit & (u >= jnp.where(me > 0, -rows, 0))
    for h in range(GROUP):
        s = lax.dot_general(
            q[:, h * HD : (h + 1) * HD],
            keys,
            (((1,), (1,)), ((), ())),
            preferred_element_type=jnp.float32,
        )
        s = jnp.where(hit, s, NEG)
        top = jnp.broadcast_to(jnp.max(s, axis=1, keepdims=True), (rows, HD))
        p = jnp.exp2((s - across(top, 2 * rows)) * SCALE2)
        m_out[h] = top
        l_out[h] = lane_sums(p)
        acc_out[h] = jnp.dot(p.astype(jnp.bfloat16), values, preferred_element_type=jnp.float32)


def across(x, width):
    return jnp.concatenate([x] * (width // HD), axis=1)


def lane_sums(p):
    total = p[:, :HD]
    for i in range(HD, p.shape[1], HD):
        total = total + p[:, i : i + HD]
    return total


def scores_of(q, h, k):
    return lax.dot_general(
        q[:, h * HD : (h + 1) * HD], k, (((1,), (1,)), ((), ())), preferred_element_type=jnp.float32
    )


def across(x, width):
    return jnp.concatenate([x] * (width // HD), axis=1)


def lane_sums(p):
    total = p[:, :HD]
    for i in range(HD, p.shape[1], HD):
        total = total + p[:, i : i + HD]
    return total


def scores_of(q, h, k):
    return lax.dot_general(
        q[:, h * HD : (h + 1) * HD], k, (((1,), (1,)), ((), ())), preferred_element_type=jnp.float32
    )


def update(scores, values, live, old, total, acc):
    masked, base = [], 0
    for s in scores:
        key = base + lax.broadcasted_iota(jnp.int32, s.shape, 1)
        masked.append(jnp.where(key < live, s, NEG))
        base += s.shape[1]
    top = functools.reduce(jnp.maximum, [jnp.max(s, axis=1, keepdims=True) for s in masked])
    top = jnp.maximum(old, jnp.broadcast_to(top, old.shape))
    factor = jnp.exp2((old - top) * SCALE2)
    total, acc = total * factor, acc * factor
    for s, v in zip(masked, values):
        p = jnp.exp2((s - across(top, s.shape[1])) * SCALE2)
        total = total + lane_sums(p)
        acc = acc + jnp.dot(p.astype(jnp.bfloat16), v, preferred_element_type=jnp.float32)
    return top, total, acc


def row_sum(total):
    return jnp.broadcast_to(jnp.sum(total, axis=1, keepdims=True), total.shape)


def each_head(tab, shift, q, lo, hi, m_in, l_in, acc_in):
    y, _ = position()
    live = ((at(tab, 32) - ((y - shift) & 3) + 3) >> 2) * BLK
    following = [scores_of(q, 0, lo[0]), scores_of(q, 0, hi[0])]
    for h in range(GROUP):
        current = following
        if h + 1 < GROUP:
            following = [scores_of(q, h + 1, lo[0]), scores_of(q, h + 1, hi[0])]
        yield h, update(current, (lo[1], hi[1]), live, m_in[h], l_in[h], acc_in[h])


def far_kernel(shift, tab, q, lo, hi, m_in, l_in, acc_in, m_out, l_out, acc_out):
    for h, new in each_head(tab, shift, q, lo, hi, m_in, l_in, acc_in):
        m_out[h], l_out[h], acc_out[h] = new


def last_kernel(shift, tab, q, lo, hi, m_in, l_in, acc_in, att):
    for h, (_, total, acc) in each_head(tab, shift, q, lo, hi, m_in, l_in, acc_in):
        att[:, h * HD : (h + 1) * HD] = (acc / row_sum(total)).astype(jnp.bfloat16)


def product_kernel(cols, att, w, out):
    out[0] = jnp.dot(att[...], w[...], preferred_element_type=jnp.float32).astype(out.dtype)


def halves_kernel(mine, recv, a, b):
    total = (mine[2] + recv[2].astype(jnp.float32)).astype(a.dtype)
    half = a.shape[0]
    a[...] = total[:half]
    b[...] = total[half:]


def pass_kernel(mine, recv, a, b, right, left):
    half = a.shape[0]
    forth = mine[1] + recv[1].astype(jnp.float32)
    back = mine[3] + recv[3].astype(jnp.float32)
    right[:half] = (forth[:half] + a[...].astype(jnp.float32)).astype(right.dtype)
    right[half:] = forth[half:].astype(right.dtype)
    left[:half] = back[:half].astype(left.dtype)
    left[half:] = (back[half:] + b[...].astype(jnp.float32)).astype(left.dtype)


def final_kernel(mine, recv, a, b, out):
    total = mine[0] + recv[0].astype(jnp.float32)
    total = total + a[...].astype(jnp.float32) + b[...].astype(jnp.float32)
    out[...] = total.astype(out.dtype)


def local(
    tokens,
    norm_gain,
    w_query,
    w_key,
    w_value,
    w_out,
    cache_keys,
    cache_values,
    vert_blocks,
    vert_count,
    slash_offsets,
    slash_count,
):
    rows = tokens.shape[0]
    bf16 = jnp.bfloat16
    f32 = jnp.float32
    blocks = vert_blocks[0]
    index = jnp.arange(128, dtype=jnp.int32)
    entry = index[:64]
    key = jnp.where(
        entry < vert_count[0],
        (((blocks >> 4) & 7) << 6) | ((blocks >> 7) << 4) | (blocks & 15),
        4096 + entry,
    )
    edges = jnp.concatenate([key, entry * 16])
    below = jnp.sum((key[None, :] < edges[:, None]).astype(jnp.int32), axis=1)
    ranked = jnp.sum(jnp.where(below[None, :64] == index[:, None], key[None, :], 0), axis=1)
    tab = jnp.where(index < 64, ranked, below)
    heads = lax.axis_index("heads")
    x, core = heads // 2, lax.rem(heads, 2)
    order = ((x + entry[:NX]) & 3) * 2
    tab, away_cols, home_cols = tie(tab, order + 1 - core, order + core)

    slot = jax.ShapeDtypeStruct((2, 2, BLK, HD), bf16)
    picked = pl.pallas_call(
        pick_kernel,
        out_shape=[slot] * NY,
        in_specs=[SSPEC, HSPEC, HSPEC],
        out_specs=[VSPEC] * NY,
        scratch_shapes=[pltpu.SemaphoreType.DMA((16,))],
        compiler_params=params(60),
        cost_estimate=cost(0.7),
        name="pick",
    )(tab, cache_keys, cache_values)
    spread = [picked[0]] + [shift_y(picked[d], d) for d in range(1, NY)]
    activation = tokens.astype(f32)
    normed = (
        activation
        * lax.rsqrt(jnp.mean(activation * activation, axis=-1, keepdims=True) + 1e-05)
        * norm_gain
    ).astype(bf16)
    spread[3], normed = tie(spread[3], normed)
    column = pl.pallas_call(
        column_kernel,
        out_shape=jax.ShapeDtypeStruct((8, 2, BLK, HD), bf16),
        in_specs=[SSPEC] + [VSPEC] * NY,
        out_specs=VSPEC,
        compiler_params=params(8),
        cost_estimate=cost(0.8),
        name="column",
    )(tab, *spread)
    key_rows = jnp.dot(normed, w_key, preferred_element_type=f32).astype(bf16)
    value_rows = jnp.dot(normed, w_value, preferred_element_type=f32).astype(bf16)
    seqs = lax.axis_size("seq")
    route = [(i, (i + 1) % seqs) for i in range(seqs)]
    ring = [column] + [None] * 7
    ring[1], ring[7] = shift_z(column, 1), shift_z(column, -1)
    ring[1], key_rows, value_rows = tie(ring[1], key_rows, value_rows)
    ring[2], ring[6] = shift_z(ring[1], 1), shift_z(ring[7], -1)
    before_keys, before_values = lax.ppermute((key_rows, value_rows), "seq", route)
    queries = jnp.dot(normed, w_query, preferred_element_type=f32).astype(bf16)
    ring[2], queries = tie(ring[2], queries)
    ring[3], ring[5] = shift_z(ring[2], 1), shift_z(ring[6], -1)
    state_shape = [jax.ShapeDtypeStruct((GROUP, rows, HD), f32)] * 3
    state = pl.pallas_call(
        near_kernel,
        out_shape=state_shape,
        in_specs=[SSPEC] * 2 + [VSPEC] * 5,
        out_specs=[VSPEC] * 3,
        compiler_params=params(16),
        cost_estimate=cost(2.2),
        name="near",
    )(slash_offsets, slash_count, queries, before_keys, before_values, key_rows, value_rows)
    ring[4] = shift_z(ring[3], 1)
    ring[4], *state = tie(ring[4], *state)
    half = jax.ShapeDtypeStruct((2, 8 * BLK, HD), bf16)
    own = pl.pallas_call(
        row_kernel,
        out_shape=[half] * 2,
        in_specs=[SSPEC] + [VSPEC] * NZ,
        out_specs=[VSPEC] * 2,
        compiler_params=params(16),
        cost_estimate=cost(1.3),
        name="row",
    )(tab, *ring)
    def far(shift, part, state):
        return pl.pallas_call(
            functools.partial(far_kernel, shift),
            out_shape=state_shape,
            in_specs=[SSPEC] + [VSPEC] * 6,
            out_specs=[VSPEC] * 3,
            compiler_params=params(16),
            cost_estimate=cost(1.8),
            name="far",
        )(tab, queries, *part, *state)

    lo1, hi3 = shift_y(own[0], 1), shift_y(own[1], -1)
    own_lo, own_hi, *state = tie(*own, *far(0, own, state))
    hi1, lo3 = shift_y(own_hi, 1), shift_y(own_lo, -1)
    lo2, hi2 = shift_y(lo1, 1), shift_y(hi3, -1)
    state = far(1, (lo1, hi1), state)
    state = far(3, (lo3, hi3), state)
    attended = pl.pallas_call(
        functools.partial(last_kernel, 2),
        out_shape=jax.ShapeDtypeStruct((rows, GROUP * HD), bf16),
        in_specs=[SSPEC] + [VSPEC] * 6,
        out_specs=VSPEC,
        compiler_params=params(16),
        cost_estimate=cost(2.5),
        name="last",
    )(tab, queries, lo2, hi2, *state)

    depth = GROUP * HD

    def product(cols, dtype):
        return pl.pallas_call(
            product_kernel,
            out_shape=jax.ShapeDtypeStruct((NX, rows, depth), dtype),
            grid_spec=pltpu.PrefetchScalarGridSpec(
                num_scalar_prefetch=1,
                grid=(NX,),
                in_specs=[
                    pl.BlockSpec((rows, depth), lambda i, cols: (0, 0)),
                    pl.BlockSpec((depth, depth), lambda i, cols: (0, cols[i])),
                ],
                out_specs=pl.BlockSpec((1, rows, depth), lambda i, cols: (i, 0, 0)),
            ),
            compiler_params=params(16),
            cost_estimate=cost(2),
            name="product",
        )(cols, attended, w_out)

    def small(kernel, count, shape, name, *operands):
        return pl.pallas_call(
            kernel,
            out_shape=[jax.ShapeDtypeStruct(shape, bf16)] * count,
            in_specs=[VSPEC] * len(operands),
            out_specs=[VSPEC] * count,
            compiler_params=params(16),
            cost_estimate=cost(0.4),
            name=name,
        )(*operands)

    away = product(away_cols, bf16)
    recv = swap_core(away)
    mine = product(home_cols, f32)
    upper, lower = small(halves_kernel, 2, (rows // 2, depth), "halves", mine, recv)
    upper, lower = shift_x(upper, 1), shift_x(lower, -1)
    right, left = small(pass_kernel, 2, (rows, depth), "pass", mine, recv, upper, lower)
    right, left = shift_x(right, 1), shift_x(left, -1)
    return small(final_kernel, 1, (rows, depth), "final", mine, recv, right, left)[0]


def solution(mesh):
    return jax.shard_map(
        local,
        mesh=mesh,
        in_specs=(
            P("seq", None),
            P(),
            P(None, "heads"),
            P(None, "heads"),
            P(None, "heads"),
            P("heads", None),
            P("heads", "seq", None),
            P("heads", "seq", None),
            P("heads", None),
            P("heads"),
            P("heads", None),
            P("heads"),
        ),
        out_specs=P("seq", "heads"),
        check_vma=False,
    )
```

```python
import functools
import math

import jax
import jax.numpy as jnp
from jax import lax
from jax.experimental import pallas as pl
from jax.experimental.pallas import tpu as pltpu
from jax.sharding import PartitionSpec as P

BLK = 64
HD = 128
GROUP = 4
NY = 4
NZ = 8
NX = 4
HALF = 4
VMEM = pltpu.VMEM
VSPEC = pl.BlockSpec(memory_space=pltpu.VMEM)
HSPEC = pl.BlockSpec(memory_space=pltpu.HBM)
SSPEC = pl.BlockSpec(memory_space=pltpu.SMEM)
SCALE2 = math.log2(math.e) / math.sqrt(HD)
NEG = -jnp.inf


def params(mib):
    return pltpu.CompilerParams(vmem_limit_bytes=mib << 20)


def cost(us):
    return pl.CostEstimate(flops=int(us * 1e9), bytes_accessed=0, transcendentals=0)


def tie(*values):
    return lax.optimization_barrier(values)


def shift_y(block, d):
    return lax.ppermute(
        block, "seq", [(y * NZ + z, (y + d) % NY * NZ + z) for y in range(NY) for z in range(NZ)]
    )


def shift_z(block, d):
    return lax.ppermute(
        block, "seq", [(y * NZ + z, y * NZ + (z + d) % NZ) for y in range(NY) for z in range(NZ)]
    )


def shift_x(block, d):
    return lax.ppermute(
        block, "heads", [(2 * x + c, 2 * ((x + d) % NX) + c) for x in range(NX) for c in range(2)]
    )


def swap_core(block):
    return lax.ppermute(block, "heads", [(i, i ^ 1) for i in range(2 * NX)])


def position():
    me = lax.axis_index("seq")
    return me // NZ, lax.rem(me, NZ)


def at(tab, group):
    return tab[64 + group]


def pick_kernel(tab, ck, cv, *refs):
    outs, sems = refs[:NY], refs[NY]
    y, z = position()
    group = z * NY + y
    start = at(tab, group)
    size = at(tab, group + 1) - start
    copies = []
    for dy in range(NY):
        for j in range(2):
            i = ((y + dy - start) & 3) + 4 * j
            entry = tab[jnp.minimum(start + i, 63)]
            row = pl.multiple_of(jnp.where(i < size, entry & 15, 0) * BLK, BLK)
            for k, cache in enumerate((ck, cv)):
                copies.append(
                    pltpu.make_async_copy(
                        cache.at[0, pl.ds(row, BLK)], outs[dy].at[j, k], sems.at[len(copies)]
                    )
                )
    for copy in copies:
        copy.start()
    for copy in copies:
        copy.wait()


def column_kernel(tab, r0, r1, r2, r3, *outs):
    y, z = position()
    recv = (r0, r1, r2, r3)
    start = at(tab, z * NY)
    size = at(tab, z * NY + NY) - start
    first = (y - start) & 3
    for i in range(8):
        off = first + 4 * i
        live = off < size
        r = jnp.minimum(start + off, 63)
        hy = (tab[r] >> 4) & 3
        j = jnp.where(live, (r - at(tab, z * NY + hy)) >> 2, 0)
        d = jnp.where(live, (y - hy) & 3, 0)
        for k in range(NY):

            @pl.when(d == k)
            def _():
                outs[i // HALF][i % HALF] = recv[k][j]


def row_kernel(tab, *refs):
    y, z = position()
    recv, outs = refs[:-2], refs[-2:]
    for m in range(16):
        r = y + 4 * m
        live = r < at(tab, 32)
        zs = jnp.where(live, tab[r] >> 6, z)
        start = at(tab, zs * NY)
        first = (y - start) & 3
        i = jnp.where(live, (r - start - first) >> 2, 0)
        source = ((z - zs) & 7) + NZ * (i // HALF)
        slot = i % HALF
        out, place = outs[m // 8], m % 8 * BLK
        for k in range(len(recv)):

            @pl.when(source == k)
            def _():
                out[0, place : place + BLK] = recv[k][slot, 0]
                out[1, place : place + BLK] = recv[k][slot, 1]


def near_kernel(offs, cnt, q, kp, vp, k, v, m_out, l_out, acc_out):
    me = lax.axis_index("seq")
    rows = k.shape[0]
    keys = jnp.concatenate([kp[...], k[...]], axis=0)
    values = jnp.concatenate([vp[...], v[...]], axis=0)
    t = lax.broadcasted_iota(jnp.int32, (rows, 2 * rows), 0)
    u = lax.broadcasted_iota(jnp.int32, (rows, 2 * rows), 1) - rows
    gap = (t >> 6) - (u >> 6)
    hit = (gap == 0) & (u <= t)
    for e in range(4):
        off = jnp.where((e < cnt[0]) & (offs[0, e] >= 0), offs[0, e], -100)
        hit = hit | (gap == off)
    hit = hit & (u >= jnp.where(me > 0, -rows, 0))
    for h in range(GROUP):
        s = lax.dot_general(
            q[:, h * HD : (h + 1) * HD],
            keys,
            (((1,), (1,)), ((), ())),
            preferred_element_type=jnp.float32,
        )
        s = jnp.where(hit, s, NEG)
        top = jnp.broadcast_to(jnp.max(s, axis=1, keepdims=True), (rows, HD))
        p = jnp.exp2((s - across(top, 2 * rows)) * SCALE2)
        m_out[h] = top
        l_out[h] = lane_sums(p)
        acc_out[h] = jnp.dot(p.astype(jnp.bfloat16), values, preferred_element_type=jnp.float32)


def across(x, width):
    return jnp.concatenate([x] * (width // HD), axis=1)


def lane_sums(p):
    total = p[:, :HD]
    for i in range(HD, p.shape[1], HD):
        total = total + p[:, i : i + HD]
    return total


def scores_of(q, h, k):
    return lax.dot_general(
        q[:, h * HD : (h + 1) * HD], k, (((1,), (1,)), ((), ())), preferred_element_type=jnp.float32
    )


def across(x, width):
    return jnp.concatenate([x] * (width // HD), axis=1)


def lane_sums(p):
    total = p[:, :HD]
    for i in range(HD, p.shape[1], HD):
        total = total + p[:, i : i + HD]
    return total


def scores_of(q, h, k):
    return lax.dot_general(
        q[:, h * HD : (h + 1) * HD], k, (((1,), (1,)), ((), ())), preferred_element_type=jnp.float32
    )


def update(scores, values, live, old, total, acc):
    masked, base = [], 0
    for s in scores:
        key = base + lax.broadcasted_iota(jnp.int32, s.shape, 1)
        masked.append(jnp.where(key < live, s, NEG))
        base += s.shape[1]
    top = functools.reduce(jnp.maximum, [jnp.max(s, axis=1, keepdims=True) for s in masked])
    top = jnp.maximum(old, jnp.broadcast_to(top, old.shape))
    factor = jnp.exp2((old - top) * SCALE2)
    total, acc = total * factor, acc * factor
    for s, v in zip(masked, values):
        p = jnp.exp2((s - across(top, s.shape[1])) * SCALE2)
        total = total + lane_sums(p)
        acc = acc + jnp.dot(p.astype(jnp.bfloat16), v, preferred_element_type=jnp.float32)
    return top, total, acc


def row_sum(total):
    return jnp.broadcast_to(jnp.sum(total, axis=1, keepdims=True), total.shape)


def each_head(tab, shift, q, lo, hi, m_in, l_in, acc_in):
    y, _ = position()
    live = ((at(tab, 32) - ((y - shift) & 3) + 3) >> 2) * BLK
    following = [scores_of(q, 0, lo[0]), scores_of(q, 0, hi[0])]
    for h in range(GROUP):
        current = following
        if h + 1 < GROUP:
            following = [scores_of(q, h + 1, lo[0]), scores_of(q, h + 1, hi[0])]
        yield h, update(current, (lo[1], hi[1]), live, m_in[h], l_in[h], acc_in[h])


def far_kernel(shift, tab, q, lo, hi, m_in, l_in, acc_in, m_out, l_out, acc_out):
    for h, new in each_head(tab, shift, q, lo, hi, m_in, l_in, acc_in):
        m_out[h], l_out[h], acc_out[h] = new


def last_kernel(shift, tab, q, lo, hi, m_in, l_in, acc_in, att):
    for h, (_, total, acc) in each_head(tab, shift, q, lo, hi, m_in, l_in, acc_in):
        att[:, h * HD : (h + 1) * HD] = (acc / row_sum(total)).astype(jnp.bfloat16)


def product_kernel(cols, att, w, out):
    out[0] = jnp.dot(att[...], w[...], preferred_element_type=jnp.float32).astype(out.dtype)


def halves_kernel(mine, recv, a, b):
    total = (mine[2] + recv[2].astype(jnp.float32)).astype(a.dtype)
    half = a.shape[0]
    a[...] = total[:half]
    b[...] = total[half:]


def pass_kernel(mine, recv, a, b, right, left):
    half = a.shape[0]
    forth = mine[1] + recv[1].astype(jnp.float32)
    back = mine[3] + recv[3].astype(jnp.float32)
    right[:half] = (forth[:half] + a[...].astype(jnp.float32)).astype(right.dtype)
    right[half:] = forth[half:].astype(right.dtype)
    left[:half] = back[:half].astype(left.dtype)
    left[half:] = (back[half:] + b[...].astype(jnp.float32)).astype(left.dtype)


def final_kernel(mine, recv, a, b, out):
    total = mine[0] + recv[0].astype(jnp.float32)
    total = total + a[...].astype(jnp.float32) + b[...].astype(jnp.float32)
    out[...] = total.astype(out.dtype)


def local(
    tokens,
    norm_gain,
    w_query,
    w_key,
    w_value,
    w_out,
    cache_keys,
    cache_values,
    vert_blocks,
    vert_count,
    slash_offsets,
    slash_count,
):
    rows = tokens.shape[0]
    bf16 = jnp.bfloat16
    f32 = jnp.float32
    blocks = vert_blocks[0]
    index = jnp.arange(128, dtype=jnp.int32)
    entry = index[:64]
    key = jnp.where(
        entry < vert_count[0],
        (((blocks >> 4) & 7) << 6) | ((blocks >> 7) << 4) | (blocks & 15),
        4096 + entry,
    )
    edges = jnp.concatenate([key, entry * 16])
    below = jnp.sum((key[None, :] < edges[:, None]).astype(jnp.int32), axis=1)
    ranked = jnp.sum(jnp.where(below[None, :64] == index[:, None], key[None, :], 0), axis=1)
    tab = jnp.where(index < 64, ranked, below)
    heads = lax.axis_index("heads")
    x, core = heads // 2, lax.rem(heads, 2)
    order = ((x + entry[:NX]) & 3) * 2
    column_ends = below[64 : 64 + 4 * NZ + 1 : 4]
    crowded = jnp.any(column_ends[1:] - column_ends[:-1] > 4 * HALF)
    tab, away_cols, home_cols, crowded = tie(tab, order + 1 - core, order + core, crowded)

    slot = jax.ShapeDtypeStruct((2, 2, BLK, HD), bf16)
    picked = pl.pallas_call(
        pick_kernel,
        out_shape=[slot] * NY,
        in_specs=[SSPEC, HSPEC, HSPEC],
        out_specs=[VSPEC] * NY,
        scratch_shapes=[pltpu.SemaphoreType.DMA((16,))],
        compiler_params=params(60),
        cost_estimate=cost(0.7),
        name="pick",
    )(tab, cache_keys, cache_values)
    spread = [picked[0]] + [shift_y(picked[d], d) for d in range(1, NY)]
    activation = tokens.astype(f32)
    normed = (
        activation
        * lax.rsqrt(jnp.mean(activation * activation, axis=-1, keepdims=True) + 1e-05)
        * norm_gain
    ).astype(bf16)
    spread[3], normed = tie(spread[3], normed)
    quarter = jax.ShapeDtypeStruct((HALF, 2, BLK, HD), bf16)
    column, rest = pl.pallas_call(
        column_kernel,
        out_shape=[quarter] * 2,
        in_specs=[SSPEC] + [VSPEC] * NY,
        out_specs=[VSPEC] * 2,
        compiler_params=params(8),
        cost_estimate=cost(0.8),
        name="column",
    )(tab, *spread)
    key_rows = jnp.dot(normed, w_key, preferred_element_type=f32).astype(bf16)
    value_rows = jnp.dot(normed, w_value, preferred_element_type=f32).astype(bf16)
    queries = jnp.dot(normed, w_query, preferred_element_type=f32).astype(bf16)
    seqs = lax.axis_size("seq")
    route = [(i, (i + 1) % seqs) for i in range(seqs)]

    def along_z(block, between=lambda x: x):
        ring = [block] + [None] * 7
        ring[2], ring[6] = shift_z(block, 2), shift_z(block, -2)
        ring[1], ring[7] = shift_z(block, 1), shift_z(block, -1)
        ring[2] = between(ring[2])
        ring[3], ring[5] = shift_z(ring[2], 1), shift_z(ring[6], -1)
        ring[4] = shift_z(ring[2], 2)
        return ring

    made = []

    def between(block):
        block, *rows_made = tie(block, key_rows, value_rows, queries)
        made.extend(rows_made)
        return block

    ring = along_z(column, between)
    key_rows, value_rows, queries = made
    before_keys, before_values = lax.ppermute((key_rows, value_rows), "seq", route)
    half = jax.ShapeDtypeStruct((2, 8 * BLK, HD), bf16)

    def compact(*sources):
        return tuple(
            pl.pallas_call(
                row_kernel,
                out_shape=[half] * 2,
                in_specs=[SSPEC] + [VSPEC] * len(sources),
                out_specs=[VSPEC] * 2,
                compiler_params=params(16),
                cost_estimate=cost(1.3),
                name="row",
            )(tab, *sources)
        )

    rest, before_keys, before_values = tie(rest, before_keys, before_values)
    own = lax.cond(
        crowded,
        lambda rest, *ring: compact(*ring, *along_z(rest)),
        lambda rest, *ring: compact(*ring),
        rest,
        *ring,
    )
    own_lo, own_hi, near_queries = tie(*own, queries)
    own = (own_lo, own_hi)
    state_shape = [jax.ShapeDtypeStruct((GROUP, rows, HD), f32)] * 3
    state = pl.pallas_call(
        near_kernel,
        out_shape=state_shape,
        in_specs=[SSPEC] * 2 + [VSPEC] * 5,
        out_specs=[VSPEC] * 3,
        compiler_params=params(16),
        cost_estimate=cost(2.2),
        name="near",
    )(slash_offsets, slash_count, near_queries, before_keys, before_values, key_rows, value_rows)

    def far(shift, part, state):
        return pl.pallas_call(
            functools.partial(far_kernel, shift),
            out_shape=state_shape,
            in_specs=[SSPEC] + [VSPEC] * 6,
            out_specs=[VSPEC] * 3,
            compiler_params=params(16),
            cost_estimate=cost(1.8),
            name="far",
        )(tab, queries, *part, *state)

    lo1, hi3 = shift_y(own[0], 1), shift_y(own[1], -1)
    own_lo, own_hi, *state = tie(*own, *far(0, own, state))
    hi1, lo3 = shift_y(own_hi, 1), shift_y(own_lo, -1)
    lo2, hi2 = shift_y(lo1, 1), shift_y(hi3, -1)
    state = far(1, (lo1, hi1), state)
    state = far(3, (lo3, hi3), state)
    attended = pl.pallas_call(
        functools.partial(last_kernel, 2),
        out_shape=jax.ShapeDtypeStruct((rows, GROUP * HD), bf16),
        in_specs=[SSPEC] + [VSPEC] * 6,
        out_specs=VSPEC,
        compiler_params=params(16),
        cost_estimate=cost(2.5),
        name="last",
    )(tab, queries, lo2, hi2, *state)

    depth = GROUP * HD

    def product(cols, dtype):
        return pl.pallas_call(
            product_kernel,
            out_shape=jax.ShapeDtypeStruct((NX, rows, depth), dtype),
            grid_spec=pltpu.PrefetchScalarGridSpec(
                num_scalar_prefetch=1,
                grid=(NX,),
                in_specs=[
                    pl.BlockSpec((rows, depth), lambda i, cols: (0, 0)),
                    pl.BlockSpec((depth, depth), lambda i, cols: (0, cols[i])),
                ],
                out_specs=pl.BlockSpec((1, rows, depth), lambda i, cols: (i, 0, 0)),
            ),
            compiler_params=params(16),
            cost_estimate=cost(2),
            name="product",
        )(cols, attended, w_out)

    def small(kernel, count, shape, name, *operands):
        return pl.pallas_call(
            kernel,
            out_shape=[jax.ShapeDtypeStruct(shape, bf16)] * count,
            in_specs=[VSPEC] * len(operands),
            out_specs=[VSPEC] * count,
            compiler_params=params(16),
            cost_estimate=cost(0.4),
            name=name,
        )(*operands)

    away = product(away_cols, bf16)
    recv = swap_core(away)
    mine = product(home_cols, f32)
    upper, lower = small(halves_kernel, 2, (rows // 2, depth), "halves", mine, recv)
    upper, lower = shift_x(upper, 1), shift_x(lower, -1)
    right, left = small(pass_kernel, 2, (rows, depth), "pass", mine, recv, upper, lower)
    right, left = shift_x(right, 1), shift_x(left, -1)
    return small(final_kernel, 1, (rows, depth), "final", mine, recv, right, left)[0]


def solution(mesh):
    return jax.shard_map(
        local,
        mesh=mesh,
        in_specs=(
            P("seq", None),
            P(),
            P(None, "heads"),
            P(None, "heads"),
            P(None, "heads"),
            P("heads", None),
            P("heads", "seq", None),
            P("heads", "seq", None),
            P("heads", None),
            P("heads"),
            P("heads", None),
            P("heads"),
        ),
        out_specs=P("seq", "heads"),
        check_vma=False,
    )
```

```python
import functools
import math

import jax
import jax.numpy as jnp
from jax import lax
from jax.experimental import pallas as pl
from jax.experimental.pallas import tpu as pltpu
from jax.sharding import PartitionSpec as P

BLK = 64
HD = 128
GROUP = 4
NY = 4
NZ = 8
NX = 4
HALF = 4
VMEM = pltpu.VMEM
VSPEC = pl.BlockSpec(memory_space=pltpu.VMEM)
HSPEC = pl.BlockSpec(memory_space=pltpu.HBM)
SSPEC = pl.BlockSpec(memory_space=pltpu.SMEM)
SCALE2 = math.log2(math.e) / math.sqrt(HD)
NEG = -jnp.inf


def params(mib):
    return pltpu.CompilerParams(vmem_limit_bytes=mib << 20)


def cost(us):
    return pl.CostEstimate(flops=int(us * 1e9), bytes_accessed=0, transcendentals=0)


def tie(*values):
    return lax.optimization_barrier(values)


def shift_y(block, d):
    return lax.ppermute(
        block, "seq", [(y * NZ + z, (y + d) % NY * NZ + z) for y in range(NY) for z in range(NZ)]
    )


def shift_z(block, d):
    return lax.ppermute(
        block, "seq", [(y * NZ + z, y * NZ + (z + d) % NZ) for y in range(NY) for z in range(NZ)]
    )


def shift_x(block, d):
    return lax.ppermute(
        block, "heads", [(2 * x + c, 2 * ((x + d) % NX) + c) for x in range(NX) for c in range(2)]
    )


def swap_core(block):
    return lax.ppermute(block, "heads", [(i, i ^ 1) for i in range(2 * NX)])


def position():
    me = lax.axis_index("seq")
    return me // NZ, lax.rem(me, NZ)


def at(tab, group):
    return tab[64 + group]


def pick_kernel(tab, ck, cv, *refs):
    outs, sems = refs[:NY], refs[NY]
    y, z = position()
    group = z * NY + y
    start = at(tab, group)
    size = at(tab, group + 1) - start
    copies = []
    for dy in range(NY):
        for j in range(2):
            i = ((y + dy - start) & 3) + 4 * j
            entry = tab[jnp.minimum(start + i, 63)]
            row = pl.multiple_of(jnp.where(i < size, entry & 15, 0) * BLK, BLK)
            for k, cache in enumerate((ck, cv)):
                copies.append(
                    pltpu.make_async_copy(
                        cache.at[0, pl.ds(row, BLK)], outs[dy].at[j, k], sems.at[len(copies)]
                    )
                )
    for copy in copies:
        copy.start()
    for copy in copies:
        copy.wait()


def column_kernel(tab, r0, r1, r2, r3, *outs):
    y, z = position()
    recv = (r0, r1, r2, r3)
    start = at(tab, z * NY)
    size = at(tab, z * NY + NY) - start
    first = (y - start) & 3
    for part, out in enumerate(outs):

        def fill(i, carry):
            off = first + 4 * (HALF * part + i)
            live = off < size
            r = jnp.minimum(start + off, 63)
            hy = (tab[r] >> 4) & 3
            j = jnp.where(live, (r - at(tab, z * NY + hy)) >> 2, 0)
            d = jnp.where(live, (y - hy) & 3, 0)
            for k in range(NY):

                @pl.when(d == k)
                def _():
                    out[i] = recv[k][j]

            return carry

        lax.fori_loop(0, HALF, fill, 0)


def row_kernel(tab, *refs):
    y, z = position()
    recv, outs = refs[:-2], refs[-2:]
    for part, out in enumerate(outs):

        def fill(m, carry):
            r = y + 4 * (8 * part + m)
            live = r < at(tab, 32)
            zs = jnp.where(live, tab[r] >> 6, z)
            start = at(tab, zs * NY)
            first = (y - start) & 3
            i = jnp.where(live, (r - start - first) >> 2, 0)
            source = ((z - zs) & 7) + NZ * (i >> 2)
            slot = i & 3
            place = pl.multiple_of(m * BLK, BLK)
            for k in range(len(recv)):

                @pl.when(source == k)
                def _():
                    out[0, pl.ds(place, BLK), :] = recv[k][slot, 0]
                    out[1, pl.ds(place, BLK), :] = recv[k][slot, 1]

            return carry

        lax.fori_loop(0, 8, fill, 0)


def near_kernel(offs, cnt, q, kp, vp, k, v, m_out, l_out, acc_out):
    me = lax.axis_index("seq")
    rows = k.shape[0]
    keys = jnp.concatenate([kp[...], k[...]], axis=0)
    values = jnp.concatenate([vp[...], v[...]], axis=0)
    t = lax.broadcasted_iota(jnp.int32, (rows, 2 * rows), 0)
    u = lax.broadcasted_iota(jnp.int32, (rows, 2 * rows), 1) - rows
    gap = (t >> 6) - (u >> 6)
    hit = (gap == 0) & (u <= t)
    for e in range(4):
        off = jnp.where((e < cnt[0]) & (offs[0, e] >= 0), offs[0, e], -100)
        hit = hit | (gap == off)
    hit = hit & (u >= jnp.where(me > 0, -rows, 0))
    for h in range(GROUP):
        s = lax.dot_general(
            q[:, h * HD : (h + 1) * HD],
            keys,
            (((1,), (1,)), ((), ())),
            preferred_element_type=jnp.float32,
        )
        s = jnp.where(hit, s, NEG)
        top = jnp.broadcast_to(jnp.max(s, axis=1, keepdims=True), (rows, HD))
        p = jnp.exp2((s - across(top, 2 * rows)) * SCALE2)
        m_out[h] = top
        l_out[h] = lane_sums(p)
        acc_out[h] = jnp.dot(p.astype(jnp.bfloat16), values, preferred_element_type=jnp.float32)


def across(x, width):
    return jnp.concatenate([x] * (width // HD), axis=1)


def lane_sums(p):
    total = p[:, :HD]
    for i in range(HD, p.shape[1], HD):
        total = total + p[:, i : i + HD]
    return total


def scores_of(q, h, k):
    return lax.dot_general(
        q[:, h * HD : (h + 1) * HD], k, (((1,), (1,)), ((), ())), preferred_element_type=jnp.float32
    )


def across(x, width):
    return jnp.concatenate([x] * (width // HD), axis=1)


def lane_sums(p):
    total = p[:, :HD]
    for i in range(HD, p.shape[1], HD):
        total = total + p[:, i : i + HD]
    return total


def scores_of(q, h, k):
    return lax.dot_general(
        q[:, h * HD : (h + 1) * HD], k, (((1,), (1,)), ((), ())), preferred_element_type=jnp.float32
    )


def update(scores, values, live, old, total, acc):
    masked, base = [], 0
    for s in scores:
        key = base + lax.broadcasted_iota(jnp.int32, s.shape, 1)
        masked.append(jnp.where(key < live, s, NEG))
        base += s.shape[1]
    top = functools.reduce(jnp.maximum, [jnp.max(s, axis=1, keepdims=True) for s in masked])
    top = jnp.maximum(old, jnp.broadcast_to(top, old.shape))
    factor = jnp.exp2((old - top) * SCALE2)
    total, acc = total * factor, acc * factor
    for s, v in zip(masked, values):
        p = jnp.exp2((s - across(top, s.shape[1])) * SCALE2)
        total = total + lane_sums(p)
        acc = acc + jnp.dot(p.astype(jnp.bfloat16), v, preferred_element_type=jnp.float32)
    return top, total, acc


def row_sum(total):
    return jnp.broadcast_to(jnp.sum(total, axis=1, keepdims=True), total.shape)


def each_head(tab, shift, q, lo, hi, m_in, l_in, acc_in):
    y, _ = position()
    live = ((at(tab, 32) - ((y - shift) & 3) + 3) >> 2) * BLK
    following = [scores_of(q, 0, lo[0]), scores_of(q, 0, hi[0])]
    for h in range(GROUP):
        current = following
        if h + 1 < GROUP:
            following = [scores_of(q, h + 1, lo[0]), scores_of(q, h + 1, hi[0])]
        yield h, update(current, (lo[1], hi[1]), live, m_in[h], l_in[h], acc_in[h])


def far_kernel(shift, tab, q, lo, hi, m_in, l_in, acc_in, m_out, l_out, acc_out):
    for h, new in each_head(tab, shift, q, lo, hi, m_in, l_in, acc_in):
        m_out[h], l_out[h], acc_out[h] = new


def last_kernel(shift, tab, q, lo, hi, m_in, l_in, acc_in, att):
    for h, (_, total, acc) in each_head(tab, shift, q, lo, hi, m_in, l_in, acc_in):
        att[:, h * HD : (h + 1) * HD] = (acc / row_sum(total)).astype(jnp.bfloat16)


def product_kernel(cols, att, w, out):
    out[0] = jnp.dot(att[...], w[...], preferred_element_type=jnp.float32).astype(out.dtype)


def halves_kernel(mine, recv, a, b):
    total = (mine[2] + recv[2].astype(jnp.float32)).astype(a.dtype)
    half = a.shape[0]
    a[...] = total[:half]
    b[...] = total[half:]


def pass_kernel(mine, recv, a, b, right, left):
    half = a.shape[0]
    forth = mine[1] + recv[1].astype(jnp.float32)
    back = mine[3] + recv[3].astype(jnp.float32)
    right[:half] = (forth[:half] + a[...].astype(jnp.float32)).astype(right.dtype)
    right[half:] = forth[half:].astype(right.dtype)
    left[:half] = back[:half].astype(left.dtype)
    left[half:] = (back[half:] + b[...].astype(jnp.float32)).astype(left.dtype)


def final_kernel(mine, recv, a, b, out):
    total = mine[0] + recv[0].astype(jnp.float32)
    total = total + a[...].astype(jnp.float32) + b[...].astype(jnp.float32)
    out[...] = total.astype(out.dtype)


def local(
    tokens,
    norm_gain,
    w_query,
    w_key,
    w_value,
    w_out,
    cache_keys,
    cache_values,
    vert_blocks,
    vert_count,
    slash_offsets,
    slash_count,
):
    rows = tokens.shape[0]
    bf16 = jnp.bfloat16
    f32 = jnp.float32
    blocks = vert_blocks[0]
    index = jnp.arange(128, dtype=jnp.int32)
    entry = index[:64]
    key = jnp.where(
        entry < vert_count[0],
        (((blocks >> 4) & 7) << 6) | ((blocks >> 7) << 4) | (blocks & 15),
        4096 + entry,
    )
    edges = jnp.concatenate([key, entry * 16])
    below = jnp.sum((key[None, :] < edges[:, None]).astype(jnp.int32), axis=1)
    ranked = jnp.sum(jnp.where(below[None, :64] == index[:, None], key[None, :], 0), axis=1)
    tab = jnp.where(index < 64, ranked, below)
    heads = lax.axis_index("heads")
    x, core = heads // 2, lax.rem(heads, 2)
    order = ((x + entry[:NX]) & 3) * 2
    column_ends = below[64 : 64 + 4 * NZ + 1 : 4]
    crowded = jnp.any(column_ends[1:] - column_ends[:-1] > 4 * HALF)
    tab, away_cols, home_cols, crowded = tie(tab, order + 1 - core, order + core, crowded)

    slot = jax.ShapeDtypeStruct((2, 2, BLK, HD), bf16)
    picked = pl.pallas_call(
        pick_kernel,
        out_shape=[slot] * NY,
        in_specs=[SSPEC, HSPEC, HSPEC],
        out_specs=[VSPEC] * NY,
        scratch_shapes=[pltpu.SemaphoreType.DMA((16,))],
        compiler_params=params(60),
        cost_estimate=cost(0.7),
        name="pick",
    )(tab, cache_keys, cache_values)
    spread = [picked[0]] + [shift_y(picked[d], d) for d in range(1, NY)]
    activation = tokens.astype(f32)
    normed = (
        activation
        * lax.rsqrt(jnp.mean(activation * activation, axis=-1, keepdims=True) + 1e-05)
        * norm_gain
    ).astype(bf16)
    spread[3], normed = tie(spread[3], normed)
    quarter = jax.ShapeDtypeStruct((HALF, 2, BLK, HD), bf16)
    column, rest = pl.pallas_call(
        column_kernel,
        out_shape=[quarter] * 2,
        in_specs=[SSPEC] + [VSPEC] * NY,
        out_specs=[VSPEC] * 2,
        compiler_params=params(8),
        cost_estimate=cost(0.8),
        name="column",
    )(tab, *spread)
    key_rows = jnp.dot(normed, w_key, preferred_element_type=f32).astype(bf16)
    value_rows = jnp.dot(normed, w_value, preferred_element_type=f32).astype(bf16)
    queries = jnp.dot(normed, w_query, preferred_element_type=f32).astype(bf16)
    seqs = lax.axis_size("seq")
    route = [(i, (i + 1) % seqs) for i in range(seqs)]

    def along_z(block, between=lambda *phase: phase):
        ring = [block] + [None] * 7
        first = [shift_z(block, d) for d in (2, -2, 1, -1)]
        ring[2], ring[6], ring[1], ring[7] = between(*first)
        ring[3], ring[5] = shift_z(ring[2], 1), shift_z(ring[6], -1)
        ring[4] = shift_z(ring[2], 2)
        return ring

    made = []

    def between(*phase):
        *phase, keys, values, rows_made = tie(*phase, key_rows, value_rows, queries)
        made.extend((keys, values, rows_made))
        return phase

    ring = along_z(column, between)
    key_rows, value_rows, queries = made
    before_keys, before_values = lax.ppermute((key_rows, value_rows), "seq", route)
    half = jax.ShapeDtypeStruct((2, 8 * BLK, HD), bf16)

    def compact(*sources):
        return tuple(
            pl.pallas_call(
                row_kernel,
                out_shape=[half] * 2,
                in_specs=[SSPEC] + [VSPEC] * len(sources),
                out_specs=[VSPEC] * 2,
                compiler_params=params(16),
                cost_estimate=cost(1.3),
                name="row",
            )(tab, *sources)
        )

    rest, before_keys, before_values = tie(rest, before_keys, before_values)
    own = lax.cond(
        crowded,
        lambda rest, *ring: compact(*ring, *along_z(rest)),
        lambda rest, *ring: compact(*ring),
        rest,
        *ring,
    )
    own_lo, own_hi, near_queries = tie(*own, queries)
    own = (own_lo, own_hi)
    state_shape = [jax.ShapeDtypeStruct((GROUP, rows, HD), f32)] * 3
    state = pl.pallas_call(
        near_kernel,
        out_shape=state_shape,
        in_specs=[SSPEC] * 2 + [VSPEC] * 5,
        out_specs=[VSPEC] * 3,
        compiler_params=params(16),
        cost_estimate=cost(2.2),
        name="near",
    )(slash_offsets, slash_count, near_queries, before_keys, before_values, key_rows, value_rows)

    def far(shift, part, state):
        return pl.pallas_call(
            functools.partial(far_kernel, shift),
            out_shape=state_shape,
            in_specs=[SSPEC] + [VSPEC] * 6,
            out_specs=[VSPEC] * 3,
            compiler_params=params(16),
            cost_estimate=cost(1.8),
            name="far",
        )(tab, queries, *part, *state)

    lo1, hi3 = shift_y(own[0], 1), shift_y(own[1], -1)
    hi1, lo3 = shift_y(own[1], 1), shift_y(own[0], -1)
    state = far(0, own, state)
    lo2, hi2 = shift_y(lo1, 1), shift_y(hi3, -1)
    state = far(1, (lo1, hi1), state)
    state = far(3, (lo3, hi3), state)
    attended = pl.pallas_call(
        functools.partial(last_kernel, 2),
        out_shape=jax.ShapeDtypeStruct((rows, GROUP * HD), bf16),
        in_specs=[SSPEC] + [VSPEC] * 6,
        out_specs=VSPEC,
        compiler_params=params(16),
        cost_estimate=cost(2.5),
        name="last",
    )(tab, queries, lo2, hi2, *state)

    depth = GROUP * HD

    def product(cols, dtype):
        return pl.pallas_call(
            product_kernel,
            out_shape=jax.ShapeDtypeStruct((NX, rows, depth), dtype),
            grid_spec=pltpu.PrefetchScalarGridSpec(
                num_scalar_prefetch=1,
                grid=(NX,),
                in_specs=[
                    pl.BlockSpec((rows, depth), lambda i, cols: (0, 0)),
                    pl.BlockSpec((depth, depth), lambda i, cols: (0, cols[i])),
                ],
                out_specs=pl.BlockSpec((1, rows, depth), lambda i, cols: (i, 0, 0)),
            ),
            compiler_params=params(16),
            cost_estimate=cost(2),
            name="product",
        )(cols, attended, w_out)

    def small(kernel, count, shape, name, *operands):
        return pl.pallas_call(
            kernel,
            out_shape=[jax.ShapeDtypeStruct(shape, bf16)] * count,
            in_specs=[VSPEC] * len(operands),
            out_specs=[VSPEC] * count,
            compiler_params=params(16),
            cost_estimate=cost(0.4),
            name=name,
        )(*operands)

    away = product(away_cols, bf16)
    recv = swap_core(away)
    mine = product(home_cols, f32)
    upper, lower = small(halves_kernel, 2, (rows // 2, depth), "halves", mine, recv)
    upper, lower = shift_x(upper, 1), shift_x(lower, -1)
    right, left = small(pass_kernel, 2, (rows, depth), "pass", mine, recv, upper, lower)
    right, left = shift_x(right, 1), shift_x(left, -1)
    return small(final_kernel, 1, (rows, depth), "final", mine, recv, right, left)[0]


def solution(mesh):
    return jax.shard_map(
        local,
        mesh=mesh,
        in_specs=(
            P("seq", None),
            P(),
            P(None, "heads"),
            P(None, "heads"),
            P(None, "heads"),
            P("heads", None),
            P("heads", "seq", None),
            P("heads", "seq", None),
            P("heads", None),
            P("heads"),
            P("heads", None),
            P("heads"),
        ),
        out_specs=P("seq", "heads"),
        check_vma=False,
    )
```

```python
import functools
import math

import jax
import jax.numpy as jnp
from jax import lax
from jax.experimental import pallas as pl
from jax.experimental.pallas import tpu as pltpu
from jax.sharding import PartitionSpec as P

BLK = 64
HD = 128
GROUP = 4
NY = 4
NZ = 8
NX = 4
HALF = 4
VMEM = pltpu.VMEM
VSPEC = pl.BlockSpec(memory_space=pltpu.VMEM)
HSPEC = pl.BlockSpec(memory_space=pltpu.HBM)
SSPEC = pl.BlockSpec(memory_space=pltpu.SMEM)
SCALE2 = math.log2(math.e) / math.sqrt(HD)
NEG = -jnp.inf


def params(mib):
    return pltpu.CompilerParams(vmem_limit_bytes=mib << 20)


def cost(us):
    return pl.CostEstimate(flops=int(us * 1e9), bytes_accessed=0, transcendentals=0)


def tie(*values):
    return lax.optimization_barrier(values)


def shift_y(block, d):
    return lax.ppermute(
        block, "seq", [(y * NZ + z, (y + d) % NY * NZ + z) for y in range(NY) for z in range(NZ)]
    )


def shift_z(block, d):
    return lax.ppermute(
        block, "seq", [(y * NZ + z, y * NZ + (z + d) % NZ) for y in range(NY) for z in range(NZ)]
    )


def shift_x(block, d):
    return lax.ppermute(
        block, "heads", [(2 * x + c, 2 * ((x + d) % NX) + c) for x in range(NX) for c in range(2)]
    )


def swap_core(block):
    return lax.ppermute(block, "heads", [(i, i ^ 1) for i in range(2 * NX)])


def position():
    me = lax.axis_index("seq")
    return me // NZ, lax.rem(me, NZ)


def at(tab, group):
    return tab[64 + group]


def pick_kernel(tab, ck, cv, *refs):
    outs, sems = refs[:NY], refs[NY]
    y, z = position()
    group = z * NY + y
    start = at(tab, group)
    size = at(tab, group + 1) - start
    copies = []
    for dy in range(NY):
        for j in range(2):
            i = ((y + dy - start) & 3) + 4 * j
            entry = tab[jnp.minimum(start + i, 63)]
            row = pl.multiple_of(jnp.where(i < size, entry & 15, 0) * BLK, BLK)
            for k, cache in enumerate((ck, cv)):
                copies.append(
                    pltpu.make_async_copy(
                        cache.at[0, pl.ds(row, BLK)], outs[dy].at[j, k], sems.at[len(copies)]
                    )
                )
    for copy in copies:
        copy.start()
    for copy in copies:
        copy.wait()


def column_kernel(tab, r0, r1, r2, r3, *outs):
    y, z = position()
    recv = (r0, r1, r2, r3)
    start = at(tab, z * NY)
    size = at(tab, z * NY + NY) - start
    first = (y - start) & 3
    for part, out in enumerate(outs):

        def fill(i, carry):
            off = first + 4 * (HALF * part + i)
            live = off < size
            r = jnp.minimum(start + off, 63)
            hy = (tab[r] >> 4) & 3
            j = jnp.where(live, (r - at(tab, z * NY + hy)) >> 2, 0)
            d = jnp.where(live, (y - hy) & 3, 0)
            for k in range(NY):

                @pl.when(d == k)
                def _():
                    out[i] = recv[k][j]

            return carry

        lax.fori_loop(0, HALF, fill, 0)


def row_kernel(tab, *refs):
    y, z = position()
    recv, outs = refs[:-2], refs[-2:]
    for part, out in enumerate(outs):

        def fill(m, carry):
            r = y + 4 * (8 * part + m)
            live = r < at(tab, 32)
            zs = jnp.where(live, tab[r] >> 6, z)
            start = at(tab, zs * NY)
            first = (y - start) & 3
            i = jnp.where(live, (r - start - first) >> 2, 0)
            source = ((z - zs) & 7) + NZ * (i >> 2)
            slot = i & 3
            place = pl.multiple_of(m * BLK, BLK)
            for k in range(len(recv)):

                @pl.when(source == k)
                def _():
                    out[0, pl.ds(place, BLK), :] = recv[k][slot, 0]
                    out[1, pl.ds(place, BLK), :] = recv[k][slot, 1]

            return carry

        lax.fori_loop(0, 8, fill, 0)


def near_kernel(offs, cnt, q, kp, vp, k, v, m_out, l_out, acc_out):
    me = lax.axis_index("seq")
    rows = k.shape[0]
    keys = jnp.concatenate([kp[...], k[...]], axis=0)
    values = jnp.concatenate([vp[...], v[...]], axis=0)
    t = lax.broadcasted_iota(jnp.int32, (rows, 2 * rows), 0)
    u = lax.broadcasted_iota(jnp.int32, (rows, 2 * rows), 1) - rows
    gap = (t >> 6) - (u >> 6)
    hit = (gap == 0) & (u <= t)
    for e in range(4):
        off = jnp.where((e < cnt[0]) & (offs[0, e] >= 0), offs[0, e], -100)
        hit = hit | (gap == off)
    hit = hit & (u >= jnp.where(me > 0, -rows, 0))
    for h in range(GROUP):
        s = lax.dot_general(
            q[:, h * HD : (h + 1) * HD],
            keys,
            (((1,), (1,)), ((), ())),
            preferred_element_type=jnp.float32,
        )
        s = jnp.where(hit, s, NEG)
        top = jnp.broadcast_to(jnp.max(s, axis=1, keepdims=True), (rows, HD))
        p = jnp.exp2((s - across(top, 2 * rows)) * SCALE2)
        m_out[h] = top
        l_out[h] = lane_sums(p)
        acc_out[h] = jnp.dot(p.astype(jnp.bfloat16), values, preferred_element_type=jnp.float32)


def across(x, width):
    return jnp.concatenate([x] * (width // HD), axis=1)


def lane_sums(p):
    total = p[:, :HD]
    for i in range(HD, p.shape[1], HD):
        total = total + p[:, i : i + HD]
    return total


def scores_of(q, h, k):
    return lax.dot_general(
        q[:, h * HD : (h + 1) * HD], k, (((1,), (1,)), ((), ())), preferred_element_type=jnp.float32
    )


def across(x, width):
    return jnp.concatenate([x] * (width // HD), axis=1)


def lane_sums(p):
    total = p[:, :HD]
    for i in range(HD, p.shape[1], HD):
        total = total + p[:, i : i + HD]
    return total


def scores_of(q, h, k):
    return lax.dot_general(
        q[:, h * HD : (h + 1) * HD], k, (((1,), (1,)), ((), ())), preferred_element_type=jnp.float32
    )


def update(scores, values, live, old, total, acc):
    masked, base = [], 0
    for s in scores:
        key = base + lax.broadcasted_iota(jnp.int32, s.shape, 1)
        masked.append(jnp.where(key < live, s, NEG))
        base += s.shape[1]
    top = functools.reduce(jnp.maximum, [jnp.max(s, axis=1, keepdims=True) for s in masked])
    top = jnp.maximum(old, jnp.broadcast_to(top, old.shape))
    factor = jnp.exp2((old - top) * SCALE2)
    total, acc = total * factor, acc * factor
    for s, v in zip(masked, values):
        p = jnp.exp2((s - across(top, s.shape[1])) * SCALE2)
        total = total + lane_sums(p)
        acc = acc + jnp.dot(p.astype(jnp.bfloat16), v, preferred_element_type=jnp.float32)
    return top, total, acc


def row_sum(total):
    return jnp.broadcast_to(jnp.sum(total, axis=1, keepdims=True), total.shape)


def each_head(tab, shift, q, lo, hi, m_in, l_in, acc_in):
    y, _ = position()
    live = ((at(tab, 32) - ((y - shift) & 3) + 3) >> 2) * BLK
    following = [scores_of(q, 0, lo[0]), scores_of(q, 0, hi[0])]
    for h in range(GROUP):
        current = following
        if h + 1 < GROUP:
            following = [scores_of(q, h + 1, lo[0]), scores_of(q, h + 1, hi[0])]
        yield h, update(current, (lo[1], hi[1]), live, m_in[h], l_in[h], acc_in[h])


def far_kernel(shift, tab, q, lo, hi, m_in, l_in, acc_in, m_out, l_out, acc_out):
    for h, new in each_head(tab, shift, q, lo, hi, m_in, l_in, acc_in):
        m_out[h], l_out[h], acc_out[h] = new


def last_kernel(shift, tab, q, lo, hi, m_in, l_in, acc_in, att):
    for h, (_, total, acc) in each_head(tab, shift, q, lo, hi, m_in, l_in, acc_in):
        att[:, h * HD : (h + 1) * HD] = (acc / row_sum(total)).astype(jnp.bfloat16)


def product_kernel(cols, att, w, out):
    out[0] = jnp.dot(att[...], w[...], preferred_element_type=jnp.float32).astype(out.dtype)


def halves_kernel(mine, recv, a, b):
    total = (mine[2] + recv[2].astype(jnp.float32)).astype(a.dtype)
    half = a.shape[0]
    a[...] = total[:half]
    b[...] = total[half:]


def pass_kernel(mine, recv, a, b, right, left):
    half = a.shape[0]
    forth = mine[1] + recv[1].astype(jnp.float32)
    back = mine[3] + recv[3].astype(jnp.float32)
    right[:half] = (forth[:half] + a[...].astype(jnp.float32)).astype(right.dtype)
    right[half:] = forth[half:].astype(right.dtype)
    left[:half] = back[:half].astype(left.dtype)
    left[half:] = (back[half:] + b[...].astype(jnp.float32)).astype(left.dtype)


def final_kernel(mine, recv, a, b, out):
    total = mine[0] + recv[0].astype(jnp.float32)
    total = total + a[...].astype(jnp.float32) + b[...].astype(jnp.float32)
    out[...] = total.astype(out.dtype)


def local(
    tokens,
    norm_gain,
    w_query,
    w_key,
    w_value,
    w_out,
    cache_keys,
    cache_values,
    vert_blocks,
    vert_count,
    slash_offsets,
    slash_count,
):
    rows = tokens.shape[0]
    bf16 = jnp.bfloat16
    f32 = jnp.float32
    blocks = vert_blocks[0]
    index = jnp.arange(128, dtype=jnp.int32)
    entry = index[:64]
    key = jnp.where(
        entry < vert_count[0],
        (((blocks >> 4) & 7) << 6) | ((blocks >> 7) << 4) | (blocks & 15),
        4096 + entry,
    )
    edges = jnp.concatenate([key, entry * 16])
    below = jnp.sum((key[None, :] < edges[:, None]).astype(jnp.int32), axis=1)
    ranked = jnp.sum(jnp.where(below[None, :64] == index[:, None], key[None, :], 0), axis=1)
    tab = jnp.where(index < 64, ranked, below)
    heads = lax.axis_index("heads")
    x, core = heads // 2, lax.rem(heads, 2)
    order = ((x + entry[:NX]) & 3) * 2
    column_ends = below[64 : 64 + 4 * NZ + 1 : 4]
    crowded = jnp.any(column_ends[1:] - column_ends[:-1] > 4 * HALF)
    tab, away_cols, home_cols, crowded = tie(tab, order + 1 - core, order + core, crowded)

    slot = jax.ShapeDtypeStruct((2, 2, BLK, HD), bf16)
    picked = pl.pallas_call(
        pick_kernel,
        out_shape=[slot] * NY,
        in_specs=[SSPEC, HSPEC, HSPEC],
        out_specs=[VSPEC] * NY,
        scratch_shapes=[pltpu.SemaphoreType.DMA((16,))],
        compiler_params=params(60),
        cost_estimate=cost(0.7),
        name="pick",
    )(tab, cache_keys, cache_values)
    spread = [picked[0]] + [shift_y(picked[d], d) for d in range(1, NY)]
    activation = tokens.astype(f32)
    normed = (
        activation
        * lax.rsqrt(jnp.mean(activation * activation, axis=-1, keepdims=True) + 1e-05)
        * norm_gain
    ).astype(bf16)
    spread[3], normed = tie(spread[3], normed)
    quarter = jax.ShapeDtypeStruct((HALF, 2, BLK, HD), bf16)
    column, rest = pl.pallas_call(
        column_kernel,
        out_shape=[quarter] * 2,
        in_specs=[SSPEC] + [VSPEC] * NY,
        out_specs=[VSPEC] * 2,
        compiler_params=params(8),
        cost_estimate=cost(0.8),
        name="column",
    )(tab, *spread)
    key_rows = jnp.dot(normed, w_key, preferred_element_type=f32).astype(bf16)
    value_rows = jnp.dot(normed, w_value, preferred_element_type=f32).astype(bf16)
    queries = jnp.dot(normed, w_query, preferred_element_type=f32).astype(bf16)
    seqs = lax.axis_size("seq")
    route = [(i, (i + 1) % seqs) for i in range(seqs)]

    def along_z(block, between=lambda *phase: phase):
        ring = [block] + [None] * 7
        first = [shift_z(block, d) for d in (2, -2, 1, -1)]
        ring[2], ring[6], ring[1], ring[7] = between(*first)
        ring[3], ring[5] = shift_z(ring[2], 1), shift_z(ring[6], -1)
        ring[4] = shift_z(ring[2], 2)
        return ring

    made, before = [], []

    def between(*phase):
        *phase, keys, values, rows_made = tie(*phase, key_rows, value_rows, queries)
        made.extend((keys, values, rows_made))
        phase[1], *arrived = tie(phase[1], *lax.ppermute((key_rows, value_rows), "seq", route))
        before.extend(arrived)
        return phase

    ring = along_z(column, between)
    key_rows, value_rows, queries = made
    before_keys, before_values = before
    half = jax.ShapeDtypeStruct((2, 8 * BLK, HD), bf16)

    def compact(*sources):
        return tuple(
            pl.pallas_call(
                row_kernel,
                out_shape=[half] * 2,
                in_specs=[SSPEC] + [VSPEC] * len(sources),
                out_specs=[VSPEC] * 2,
                compiler_params=params(16),
                cost_estimate=cost(1.3),
                name="row",
            )(tab, *sources)
        )

    own = lax.cond(
        crowded,
        lambda rest, *ring: compact(*ring, *along_z(rest)),
        lambda rest, *ring: compact(*ring),
        rest,
        *ring,
    )
    own_lo, own_hi, near_queries = tie(*own, queries)
    own = (own_lo, own_hi)
    state_shape = [jax.ShapeDtypeStruct((GROUP, rows, HD), f32)] * 3
    state = pl.pallas_call(
        near_kernel,
        out_shape=state_shape,
        in_specs=[SSPEC] * 2 + [VSPEC] * 5,
        out_specs=[VSPEC] * 3,
        compiler_params=params(16),
        cost_estimate=cost(2.2),
        name="near",
    )(slash_offsets, slash_count, near_queries, before_keys, before_values, key_rows, value_rows)

    def far(shift, part, state):
        return pl.pallas_call(
            functools.partial(far_kernel, shift),
            out_shape=state_shape,
            in_specs=[SSPEC] + [VSPEC] * 6,
            out_specs=[VSPEC] * 3,
            compiler_params=params(16),
            cost_estimate=cost(1.8),
            name="far",
        )(tab, queries, *part, *state)

    lo1, hi3 = shift_y(own[0], 1), shift_y(own[1], -1)
    hi1, lo3 = shift_y(own[1], 1), shift_y(own[0], -1)
    state = far(0, own, state)
    lo2, hi2 = shift_y(lo1, 1), shift_y(hi3, -1)
    state = far(1, (lo1, hi1), state)
    state = far(3, (lo3, hi3), state)
    attended = pl.pallas_call(
        functools.partial(last_kernel, 2),
        out_shape=jax.ShapeDtypeStruct((rows, GROUP * HD), bf16),
        in_specs=[SSPEC] + [VSPEC] * 6,
        out_specs=VSPEC,
        compiler_params=params(16),
        cost_estimate=cost(2.5),
        name="last",
    )(tab, queries, lo2, hi2, *state)

    depth = GROUP * HD

    def product(cols, dtype):
        return pl.pallas_call(
            product_kernel,
            out_shape=jax.ShapeDtypeStruct((NX, rows, depth), dtype),
            grid_spec=pltpu.PrefetchScalarGridSpec(
                num_scalar_prefetch=1,
                grid=(NX,),
                in_specs=[
                    pl.BlockSpec((rows, depth), lambda i, cols: (0, 0)),
                    pl.BlockSpec((depth, depth), lambda i, cols: (0, cols[i])),
                ],
                out_specs=pl.BlockSpec((1, rows, depth), lambda i, cols: (i, 0, 0)),
            ),
            compiler_params=params(16),
            cost_estimate=cost(2),
            name="product",
        )(cols, attended, w_out)

    def small(kernel, count, shape, name, *operands):
        return pl.pallas_call(
            kernel,
            out_shape=[jax.ShapeDtypeStruct(shape, bf16)] * count,
            in_specs=[VSPEC] * len(operands),
            out_specs=[VSPEC] * count,
            compiler_params=params(16),
            cost_estimate=cost(0.4),
            name=name,
        )(*operands)

    away = product(away_cols, bf16)
    recv = swap_core(away)
    mine = product(home_cols, f32)
    upper, lower = small(halves_kernel, 2, (rows // 2, depth), "halves", mine, recv)
    upper, lower = shift_x(upper, 1), shift_x(lower, -1)
    right, left = small(pass_kernel, 2, (rows, depth), "pass", mine, recv, upper, lower)
    right, left = shift_x(right, 1), shift_x(left, -1)
    return small(final_kernel, 1, (rows, depth), "final", mine, recv, right, left)[0]


def solution(mesh):
    return jax.shard_map(
        local,
        mesh=mesh,
        in_specs=(
            P("seq", None),
            P(),
            P(None, "heads"),
            P(None, "heads"),
            P(None, "heads"),
            P("heads", None),
            P("heads", "seq", None),
            P("heads", "seq", None),
            P("heads", None),
            P("heads"),
            P("heads", None),
            P("heads"),
        ),
        out_specs=P("seq", "heads"),
        check_vma=False,
    )
```

```python
import functools
import math

import jax
import jax.numpy as jnp
from jax import lax
from jax.experimental import pallas as pl
from jax.experimental.pallas import tpu as pltpu
from jax.sharding import PartitionSpec as P

BLK = 64
HD = 128
GROUP = 4
NY = 4
NZ = 8
NX = 4
HALF = 4
VMEM = pltpu.VMEM
VSPEC = pl.BlockSpec(memory_space=pltpu.VMEM)
HSPEC = pl.BlockSpec(memory_space=pltpu.HBM)
SSPEC = pl.BlockSpec(memory_space=pltpu.SMEM)
SCALE2 = math.log2(math.e) / math.sqrt(HD)
NEG = -jnp.inf


def params(mib):
    return pltpu.CompilerParams(vmem_limit_bytes=mib << 20)


def cost(us):
    return pl.CostEstimate(flops=int(us * 1e9), bytes_accessed=0, transcendentals=0)


def tie(*values):
    return lax.optimization_barrier(values)


def shift_y(block, d):
    return lax.ppermute(
        block, "seq", [(y * NZ + z, (y + d) % NY * NZ + z) for y in range(NY) for z in range(NZ)]
    )


def shift_z(block, d):
    return lax.ppermute(
        block, "seq", [(y * NZ + z, y * NZ + (z + d) % NZ) for y in range(NY) for z in range(NZ)]
    )


def shift_x(block, d):
    return lax.ppermute(
        block, "heads", [(2 * x + c, 2 * ((x + d) % NX) + c) for x in range(NX) for c in range(2)]
    )


def swap_core(block):
    return lax.ppermute(block, "heads", [(i, i ^ 1) for i in range(2 * NX)])


def position():
    me = lax.axis_index("seq")
    return me // NZ, lax.rem(me, NZ)


def at(tab, group):
    return tab[64 + group]


def pick_kernel(tab, ck, cv, *refs):
    outs, sems = refs[:NY], refs[NY]
    y, z = position()
    group = z * NY + y
    start = at(tab, group)
    size = at(tab, group + 1) - start
    copies = []
    for dy in range(NY):
        for j in range(2):
            i = ((y + dy - start) & 3) + 4 * j
            entry = tab[jnp.minimum(start + i, 63)]
            row = pl.multiple_of(jnp.where(i < size, entry & 15, 0) * BLK, BLK)
            for k, cache in enumerate((ck, cv)):
                copies.append(
                    pltpu.make_async_copy(
                        cache.at[0, pl.ds(row, BLK)], outs[dy].at[j, k], sems.at[len(copies)]
                    )
                )
    for copy in copies:
        copy.start()
    for copy in copies:
        copy.wait()


def column_kernel(tab, r0, r1, r2, r3, *outs):
    y, z = position()
    recv = (r0, r1, r2, r3)
    start = at(tab, z * NY)
    size = at(tab, z * NY + NY) - start
    first = (y - start) & 3
    for part, out in enumerate(outs):

        def fill(i, carry):
            off = first + 4 * (HALF * part + i)
            live = off < size
            r = jnp.minimum(start + off, 63)
            hy = (tab[r] >> 4) & 3
            j = jnp.where(live, (r - at(tab, z * NY + hy)) >> 2, 0)
            d = jnp.where(live, (y - hy) & 3, 0)
            for k in range(NY):

                @pl.when(d == k)
                def _():
                    out[i] = recv[k][j]

            return carry

        lax.fori_loop(0, HALF, fill, 0)


def row_kernel(tab, *refs):
    y, z = position()
    recv, outs = refs[:-2], refs[-2:]
    for part, out in enumerate(outs):

        def fill(m, carry):
            r = y + 4 * (8 * part + m)
            live = r < at(tab, 32)
            zs = jnp.where(live, tab[r] >> 6, z)
            start = at(tab, zs * NY)
            first = (y - start) & 3
            i = jnp.where(live, (r - start - first) >> 2, 0)
            source = ((z - zs) & 7) + NZ * (i >> 2)
            slot = i & 3
            place = pl.multiple_of(m * BLK, BLK)
            for k in range(len(recv)):

                @pl.when(source == k)
                def _():
                    out[0, pl.ds(place, BLK), :] = recv[k][slot, 0]
                    out[1, pl.ds(place, BLK), :] = recv[k][slot, 1]

            return carry

        lax.fori_loop(0, 8, fill, 0)


def near_kernel(offs, cnt, q, kp, vp, k, v, m_out, l_out, acc_out):
    me = lax.axis_index("seq")
    rows = k.shape[0]
    keys = jnp.concatenate([kp[...], k[...]], axis=0)
    values = jnp.concatenate([vp[...], v[...]], axis=0)
    t = lax.broadcasted_iota(jnp.int32, (rows, 2 * rows), 0)
    u = lax.broadcasted_iota(jnp.int32, (rows, 2 * rows), 1) - rows
    gap = (t >> 6) - (u >> 6)
    hit = (gap == 0) & (u <= t)
    for e in range(4):
        off = jnp.where((e < cnt[0]) & (offs[0, e] >= 0), offs[0, e], -100)
        hit = hit | (gap == off)
    hit = hit & (u >= jnp.where(me > 0, -rows, 0))
    for h in range(GROUP):
        s = lax.dot_general(
            q[:, h * HD : (h + 1) * HD],
            keys,
            (((1,), (1,)), ((), ())),
            preferred_element_type=jnp.float32,
        )
        s = jnp.where(hit, s, NEG)
        top = jnp.broadcast_to(jnp.max(s, axis=1, keepdims=True), (rows, HD))
        p = jnp.exp2((s - across(top, 2 * rows)) * SCALE2)
        m_out[h] = top
        l_out[h] = lane_sums(p)
        acc_out[h] = jnp.dot(p.astype(jnp.bfloat16), values, preferred_element_type=jnp.float32)


def across(x, width):
    return jnp.concatenate([x] * (width // HD), axis=1)


def lane_sums(p):
    total = p[:, :HD]
    for i in range(HD, p.shape[1], HD):
        total = total + p[:, i : i + HD]
    return total


def scores_of(q, h, k):
    return lax.dot_general(
        q[:, h * HD : (h + 1) * HD], k, (((1,), (1,)), ((), ())), preferred_element_type=jnp.float32
    )


def across(x, width):
    return jnp.concatenate([x] * (width // HD), axis=1)


def lane_sums(p):
    total = p[:, :HD]
    for i in range(HD, p.shape[1], HD):
        total = total + p[:, i : i + HD]
    return total


def scores_of(q, h, k):
    return lax.dot_general(
        q[:, h * HD : (h + 1) * HD], k, (((1,), (1,)), ((), ())), preferred_element_type=jnp.float32
    )


def update(scores, values, live, old, total, acc):
    masked, base = [], 0
    for s in scores:
        key = base + lax.broadcasted_iota(jnp.int32, s.shape, 1)
        masked.append(jnp.where(key < live, s, NEG))
        base += s.shape[1]
    top = functools.reduce(jnp.maximum, [jnp.max(s, axis=1, keepdims=True) for s in masked])
    top = jnp.maximum(old, jnp.broadcast_to(top, old.shape))
    factor = jnp.exp2((old - top) * SCALE2)
    total, acc = total * factor, acc * factor
    for s, v in zip(masked, values):
        p = jnp.exp2((s - across(top, s.shape[1])) * SCALE2)
        total = total + lane_sums(p)
        acc = acc + jnp.dot(p.astype(jnp.bfloat16), v, preferred_element_type=jnp.float32)
    return top, total, acc


def row_sum(total):
    return jnp.broadcast_to(jnp.sum(total, axis=1, keepdims=True), total.shape)


def each_head(tab, shift, q, lo, hi, m_in, l_in, acc_in):
    y, _ = position()
    live = ((at(tab, 32) - ((y - shift) & 3) + 3) >> 2) * BLK
    following = [scores_of(q, 0, lo[0]), scores_of(q, 0, hi[0])]
    for h in range(GROUP):
        current = following
        if h + 1 < GROUP:
            following = [scores_of(q, h + 1, lo[0]), scores_of(q, h + 1, hi[0])]
        yield h, update(current, (lo[1], hi[1]), live, m_in[h], l_in[h], acc_in[h])


def far_kernel(shift, tab, q, lo, hi, m_in, l_in, acc_in, m_out, l_out, acc_out):
    for h, new in each_head(tab, shift, q, lo, hi, m_in, l_in, acc_in):
        m_out[h], l_out[h], acc_out[h] = new


def last_kernel(shift, tab, q, lo, hi, m_in, l_in, acc_in, att):
    for h, (_, total, acc) in each_head(tab, shift, q, lo, hi, m_in, l_in, acc_in):
        att[:, h * HD : (h + 1) * HD] = (acc / row_sum(total)).astype(jnp.bfloat16)


def product_kernel(cols, att, w, out):
    out[0] = jnp.dot(att[...], w[...], preferred_element_type=jnp.float32).astype(out.dtype)


def halves_kernel(mine, recv, a, b):
    total = (mine[2] + recv[2].astype(jnp.float32)).astype(a.dtype)
    half = a.shape[0]
    a[...] = total[:half]
    b[...] = total[half:]


def pass_kernel(mine, recv, a, b, right, left):
    half = a.shape[0]
    forth = mine[1] + recv[1].astype(jnp.float32)
    back = mine[3] + recv[3].astype(jnp.float32)
    right[:half] = (forth[:half] + a[...].astype(jnp.float32)).astype(right.dtype)
    right[half:] = forth[half:].astype(right.dtype)
    left[:half] = back[:half].astype(left.dtype)
    left[half:] = (back[half:] + b[...].astype(jnp.float32)).astype(left.dtype)


def final_kernel(mine, recv, a, b, out):
    total = mine[0] + recv[0].astype(jnp.float32)
    total = total + a[...].astype(jnp.float32) + b[...].astype(jnp.float32)
    out[...] = total.astype(out.dtype)


def local(
    tokens,
    norm_gain,
    w_query,
    w_key,
    w_value,
    w_out,
    cache_keys,
    cache_values,
    vert_blocks,
    vert_count,
    slash_offsets,
    slash_count,
):
    rows = tokens.shape[0]
    bf16 = jnp.bfloat16
    f32 = jnp.float32
    blocks = vert_blocks[0]
    index = jnp.arange(128, dtype=jnp.int32)
    entry = index[:64]
    key = jnp.where(
        entry < vert_count[0],
        (((blocks >> 4) & 7) << 6) | ((blocks >> 7) << 4) | (blocks & 15),
        4096 + entry,
    )
    edges = jnp.concatenate([key, entry * 16])
    below = jnp.sum((key[None, :] < edges[:, None]).astype(jnp.int32), axis=1)
    ranked = jnp.sum(jnp.where(below[None, :64] == index[:, None], key[None, :], 0), axis=1)
    tab = jnp.where(index < 64, ranked, below)
    heads = lax.axis_index("heads")
    x, core = heads // 2, lax.rem(heads, 2)
    order = ((x + entry[:NX]) & 3) * 2
    column_ends = below[64 : 64 + 4 * NZ + 1 : 4]
    crowded = jnp.any(column_ends[1:] - column_ends[:-1] > 4 * HALF)
    tab, away_cols, home_cols, crowded = tie(tab, order + 1 - core, order + core, crowded)

    slot = jax.ShapeDtypeStruct((2, 2, BLK, HD), bf16)
    picked = pl.pallas_call(
        pick_kernel,
        out_shape=[slot] * NY,
        in_specs=[SSPEC, HSPEC, HSPEC],
        out_specs=[VSPEC] * NY,
        scratch_shapes=[pltpu.SemaphoreType.DMA((16,))],
        compiler_params=params(60),
        cost_estimate=cost(0.7),
        name="pick",
    )(tab, cache_keys, cache_values)
    spread = [picked[0]] + [shift_y(picked[d], d) for d in range(1, NY)]
    activation = tokens.astype(f32)
    normed = (
        activation
        * lax.rsqrt(jnp.mean(activation * activation, axis=-1, keepdims=True) + 1e-05)
        * norm_gain
    ).astype(bf16)
    spread[3], normed = tie(spread[3], normed)
    quarter = jax.ShapeDtypeStruct((HALF, 2, BLK, HD), bf16)
    column, rest = pl.pallas_call(
        column_kernel,
        out_shape=[quarter] * 2,
        in_specs=[SSPEC] + [VSPEC] * NY,
        out_specs=[VSPEC] * 2,
        compiler_params=params(8),
        cost_estimate=cost(0.8),
        name="column",
    )(tab, *spread)
    key_rows = jnp.dot(normed, w_key, preferred_element_type=f32).astype(bf16)
    value_rows = jnp.dot(normed, w_value, preferred_element_type=f32).astype(bf16)
    queries = jnp.dot(normed, w_query, preferred_element_type=f32).astype(bf16)
    seqs = lax.axis_size("seq")
    route = [(i, (i + 1) % seqs) for i in range(seqs)]

    def along_z(block, between=lambda *phase: phase):
        ring = [block] + [None] * 7
        first = [shift_z(block, d) for d in (2, -2, 1, -1)]
        ring[2], ring[6], ring[1], ring[7] = between(*first)
        ring[3], ring[5] = shift_z(ring[2], 1), shift_z(ring[6], -1)
        ring[4] = shift_z(ring[2], 2)
        return ring

    made, before = [], []

    def between(*phase):
        *phase, keys, values, rows_made = tie(*phase, key_rows, value_rows, queries)
        made.extend((keys, values, rows_made))
        phase[1], *arrived = tie(phase[1], *lax.ppermute((key_rows, value_rows), "seq", route))
        before.extend(arrived)
        return phase

    ring = along_z(column, between)
    key_rows, value_rows, queries = made
    before_keys, before_values = before
    half = jax.ShapeDtypeStruct((2, 8 * BLK, HD), bf16)

    def compact(*sources):
        return tuple(
            pl.pallas_call(
                row_kernel,
                out_shape=[half] * 2,
                in_specs=[SSPEC] + [VSPEC] * len(sources),
                out_specs=[VSPEC] * 2,
                compiler_params=params(16),
                cost_estimate=cost(1.3),
                name="row",
            )(tab, *sources)
        )

    own = lax.cond(
        crowded,
        lambda rest, *ring: compact(*ring, *along_z(rest)),
        lambda rest, *ring: compact(*ring),
        rest,
        *ring,
    )
    own_lo, own_hi, near_queries = tie(*own, queries)
    own = (own_lo, own_hi)
    state_shape = [jax.ShapeDtypeStruct((GROUP, rows, HD), f32)] * 3
    state = pl.pallas_call(
        near_kernel,
        out_shape=state_shape,
        in_specs=[SSPEC] * 2 + [VSPEC] * 5,
        out_specs=[VSPEC] * 3,
        compiler_params=params(16),
        cost_estimate=cost(2.2),
        name="near",
    )(slash_offsets, slash_count, near_queries, before_keys, before_values, key_rows, value_rows)

    def far(shift, part, state):
        return pl.pallas_call(
            functools.partial(far_kernel, shift),
            out_shape=state_shape,
            in_specs=[SSPEC] + [VSPEC] * 6,
            out_specs=[VSPEC] * 3,
            compiler_params=params(16),
            cost_estimate=cost(1.8),
            name="far",
        )(tab, queries, *part, *state)

    lo1, hi3 = shift_y(own[0], 1), shift_y(own[1], -1)
    late_lo, late_hi, *state = tie(*own, *state)
    hi1, lo3 = shift_y(late_hi, 1), shift_y(late_lo, -1)
    state = far(0, own, state)
    lo2, hi2 = shift_y(lo1, 1), shift_y(hi3, -1)
    state = far(1, (lo1, hi1), state)
    state = far(3, (lo3, hi3), state)
    attended = pl.pallas_call(
        functools.partial(last_kernel, 2),
        out_shape=jax.ShapeDtypeStruct((rows, GROUP * HD), bf16),
        in_specs=[SSPEC] + [VSPEC] * 6,
        out_specs=VSPEC,
        compiler_params=params(16),
        cost_estimate=cost(2.5),
        name="last",
    )(tab, queries, lo2, hi2, *state)

    depth = GROUP * HD

    def product(cols, dtype):
        return pl.pallas_call(
            product_kernel,
            out_shape=jax.ShapeDtypeStruct((NX, rows, depth), dtype),
            grid_spec=pltpu.PrefetchScalarGridSpec(
                num_scalar_prefetch=1,
                grid=(NX,),
                in_specs=[
                    pl.BlockSpec((rows, depth), lambda i, cols: (0, 0)),
                    pl.BlockSpec((depth, depth), lambda i, cols: (0, cols[i])),
                ],
                out_specs=pl.BlockSpec((1, rows, depth), lambda i, cols: (i, 0, 0)),
            ),
            compiler_params=params(16),
            cost_estimate=cost(2),
            name="product",
        )(cols, attended, w_out)

    def small(kernel, count, shape, name, *operands):
        return pl.pallas_call(
            kernel,
            out_shape=[jax.ShapeDtypeStruct(shape, bf16)] * count,
            in_specs=[VSPEC] * len(operands),
            out_specs=[VSPEC] * count,
            compiler_params=params(16),
            cost_estimate=cost(0.4),
            name=name,
        )(*operands)

    away = product(away_cols, bf16)
    recv = swap_core(away)
    mine = product(home_cols, f32)
    upper, lower = small(halves_kernel, 2, (rows // 2, depth), "halves", mine, recv)
    upper, lower = shift_x(upper, 1), shift_x(lower, -1)
    right, left = small(pass_kernel, 2, (rows, depth), "pass", mine, recv, upper, lower)
    right, left = shift_x(right, 1), shift_x(left, -1)
    return small(final_kernel, 1, (rows, depth), "final", mine, recv, right, left)[0]


def solution(mesh):
    return jax.shard_map(
        local,
        mesh=mesh,
        in_specs=(
            P("seq", None),
            P(),
            P(None, "heads"),
            P(None, "heads"),
            P(None, "heads"),
            P("heads", None),
            P("heads", "seq", None),
            P("heads", "seq", None),
            P("heads", None),
            P("heads"),
            P("heads", None),
            P("heads"),
        ),
        out_specs=P("seq", "heads"),
        check_vma=False,
    )
```
